128 devices in a mesh: sample: 16 (over x, z_lo, core), ctx: 8 (over y, z_hi).
Axes of the slice: x: 4, y: 4, z: 4 (z_hi: 2, z_lo: 2; z = z_hi * 2 + z_lo), core: 2. Of those that a mesh axis runs over, the one named last changes fastest.
Arguments:
- prompt_query: bfloat16 [4096, 1024], P(('sample', 'ctx')), may hold values from -13 to 13
- prompt_key: bfloat16 [4096, 128], P('ctx'), may hold values from -13 to 13
- prompt_value: bfloat16 [4096, 128], P('ctx'), may hold values from -6 to 6
- prompt_cotangent: bfloat16 [4096, 1024], P(('sample', 'ctx')), may hold values from -96 to 96
- prompt_output: bfloat16 [4096, 1024], P(('sample', 'ctx')), may hold values from -1.5 to 1.5
- response_query: bfloat16 [16, 2048, 1024], P('sample', 'ctx'), may hold values from -13 to 13
- response_key: bfloat16 [16, 2048, 128], P('sample', 'ctx'), may hold values from -6 to 6
- response_value: bfloat16 [16, 2048, 128], P('sample', 'ctx'), may hold values from -6 to 6
- response_cotangent: bfloat16 [16, 2048, 1024], P('sample', 'ctx'), may hold values from -96 to 96
- response_output: bfloat16 [16, 2048, 1024], P('sample', 'ctx'), may hold values from -1.5 to 1.5
- lengths: int32 [16], P('sample'), may hold values from 1 to 2048, 16384 in all
Outputs:
- prompt_query_grad: bfloat16 [4096, 1024], P(('sample', 'ctx'))
- prompt_key_grad: bfloat16 [4096, 128], P(('sample', 'ctx'))
- prompt_value_grad: bfloat16 [4096, 128], P(('sample', 'ctx'))
- response_query_grad: bfloat16 [16, 2048, 1024], P('sample', 'ctx')
- response_key_grad: bfloat16 [16, 2048, 128], P('sample', 'ctx')
- response_value_grad: bfloat16 [16, 2048, 128], P('sample', 'ctx')
The draws below stay inside these ranges and needn't reach their ends.
Inputs may be any that keep to these rules, and one draw needn't show every extreme that they name: The 16 lengths sum to 16384 and one of them equals 2048.
All inputs are finite; a program needn't handle non-finite values. No bound on the sum of `lengths` on one device may be relied on, other than what follows from the above.
Results may differ from the reference program's by a relative error of at most 0.015.
Values may be sent and summed in bfloat16 or wider, within the bound.
A program may use at most 64 MiB of HBM per device.

```python
import math
import jax
import jax.numpy as jnp
import numpy as np
from jax import lax

H = 8
DH = 128
PROMPT = 4096
LENGTH = 2048
RESP = 16


def draw_prompt_key(key, part):
    key = jax.random.fold_in(key, 11)
    return jax.random.truncated_normal(key, -6.0, 6.0, (PROMPT, DH), jnp.float32).astype(jnp.bfloat16)


def draw_prompt_query(key, part):
    key = jax.random.fold_in(key, 12)
    return jax.random.truncated_normal(key, -6.0, 6.0, (PROMPT, H * DH), jnp.float32).astype(jnp.bfloat16)


def draw_response_query(key, part):
    key = jax.random.fold_in(key, 13)
    return jax.random.truncated_normal(key, -6.0, 6.0, (RESP, LENGTH, H * DH), jnp.float32).astype(jnp.bfloat16)


def steps_of(key, extent, pieces, smallest, high):
    def one(axis_at, parts):
        draws = jax.random.uniform(jax.random.fold_in(jax.random.fold_in(key, 6), axis_at), (parts,), jnp.float32, smallest / len(pieces), high / len(pieces))
        return jnp.repeat(jnp.exp(draws), extent[axis_at] // parts).reshape((-1,) + (1,) * (len(extent) - axis_at - 1))

    gain = one(*pieces[0])
    for cut in pieces[1:]:
        gain = gain * one(*cut)
    return gain


def length_profile(count, total, bound, skew):
    loads = [(1 << 20) // math.isqrt(standing ** skew) + 1 for standing in range(2, count + 1)]
    surplus, holding = total - bound - (count - 1), [1] * (count - 1)
    while surplus > 0:
        candidates = [i for i in range(count - 1) if holding[i] < bound]
        whole, budget = sum([loads[i] for i in candidates]), surplus
        for i in candidates:
            extra = min(bound - holding[i], max(1, budget * loads[i] // whole), surplus)
            holding[i] = holding[i] + extra
            surplus = surplus - extra
    return np.array([bound] + holding)


def ragged(own_key, amount, total, reach, skew):
    if amount == 2:
        one = jax.random.randint(own_key, (), max(1, total - reach), min(reach, total - 1) + 1)
        return jnp.stack([one, total - one])
    sizes = jnp.asarray(length_profile(amount, total, reach, skew), jnp.int32)
    couples = (amount - 1) // 2
    source_of, taker = sizes[1:1 + 2 * couples:2], sizes[2:2 + 2 * couples:2]
    margin = jnp.minimum(source_of - 1, reach - taker)
    passed = jax.random.randint(jax.random.fold_in(own_key, 1), (couples,), 0, 1 << 20) % (margin + 1)
    sizes = sizes.at[1:1 + 2 * couples:2].set(source_of - passed).at[2:2 + 2 * couples:2].set(taker + passed)
    return sizes[jax.random.permutation(jax.random.fold_in(own_key, 2), amount)]


def bell_draw(own_key, dims, scale, bound, split=(), dtype=jnp.bfloat16):
    drawn = scale * jax.random.normal(own_key, dims, jnp.float32)
    if split:
        drawn = drawn * steps_of(own_key, dims, split, -0.22, 0.18)
    return jnp.clip(drawn, -bound, bound).astype(dtype)


def setup_inputs(seed: int = 0) -> dict:
    streams_of = jax.random.split(jax.random.key(seed), 12)
    prompt_query = draw_prompt_query(jax.random.fold_in(streams_of[11], 71), 0)
    prompt_key = draw_prompt_key(jax.random.fold_in(streams_of[11], 71), 0)
    prompt_value = bell_draw(streams_of[2], (PROMPT, DH), 1.0, 6.0, ((0, 8),))
    prompt_cotangent = bell_draw(streams_of[3], (PROMPT, H * DH), 16.0, 96.0, ((0, 128),))
    prompt_output = bell_draw(streams_of[4], (PROMPT, H * DH), 0.25, 1.5, ((0, 128),))
    response_query = draw_response_query(jax.random.fold_in(streams_of[11], 71), 0)
    response_key = bell_draw(streams_of[6], (RESP, LENGTH, DH), 1.0, 6.0, ((0, 16), (1, 8)))
    response_value = bell_draw(streams_of[7], (RESP, LENGTH, DH), 1.0, 6.0, ((0, 16), (1, 8)))
    response_cotangent = bell_draw(streams_of[8], (RESP, LENGTH, H * DH), 16.0, 96.0, ((0, 16), (1, 8)))
    response_output = bell_draw(streams_of[9], (RESP, LENGTH, H * DH), 0.25, 1.5, ((0, 16), (1, 8)))
    lengths = ragged(streams_of[10], RESP, RESP * LENGTH // 2, LENGTH, 1).astype(jnp.int32)
    return dict(prompt_query=prompt_query, prompt_key=prompt_key, prompt_value=prompt_value, prompt_cotangent=prompt_cotangent, prompt_output=prompt_output, response_query=response_query, response_key=response_key, response_value=response_value, response_cotangent=response_cotangent, response_output=response_output, lengths=lengths)


masked_value = -1.0e30


def scores_of(queries, key_rows):
    scaling = key_rows.shape[1] ** -0.5
    return jnp.einsum("nhd,md->hnm", queries.astype(jnp.float32), key_rows.astype(jnp.float32)) * scaling


def attend_back(queries, grad_out, outputs, key_rows, values, allowed, live_rows):
    scaling = key_rows.shape[1] ** -0.5
    mask = allowed[None]
    scores = jnp.where(mask, scores_of(queries, key_rows), masked_value)
    row_max = jnp.max(scores, axis=2, keepdims=True)
    weights = jnp.where(mask, jnp.exp(scores - row_max), 0.0)
    row_sum = jnp.sum(weights, axis=2, keepdims=True)
    probability = weights / row_sum * live_rows[None, :, None]
    rounded = lax.optimization_barrier(probability.astype(jnp.bfloat16))
    prob_grad = jnp.einsum("nhd,md->hnm", grad_out.astype(jnp.float32), values.astype(jnp.float32))
    row_delta = jnp.sum(grad_out.astype(jnp.float32) * outputs.astype(jnp.float32), axis=2).T[:, :, None]
    score_grad = lax.optimization_barrier((probability * (prob_grad - row_delta) * scaling).astype(jnp.bfloat16))
    query_grad = jnp.einsum("hnm,md->nhd", score_grad.astype(jnp.float32), key_rows.astype(jnp.float32))
    key_part = jnp.einsum("hnm,nhd->md", score_grad.astype(jnp.float32), queries.astype(jnp.float32))
    value_part = jnp.einsum("hnm,nhd->md", rounded.astype(jnp.float32), grad_out.astype(jnp.float32))
    return query_grad, key_part, value_part


def reference(prompt_query, prompt_key, prompt_value, prompt_cotangent, prompt_output, response_query, response_key, response_value, response_cotangent, response_output, lengths):
    prompt_block = min(512, PROMPT)
    prompt_steps = PROMPT // prompt_block
    zeros_prompt = jnp.zeros((PROMPT, DH), jnp.float32)

    def prompt_step(state_now, inputs):
        step_id, queries, grad_out, outputs = inputs
        row_ids = step_id * prompt_block + jnp.arange(prompt_block)
        allowed = jnp.arange(PROMPT)[None, :] <= row_ids[:, None]
        live_rows = jnp.ones((prompt_block,), jnp.float32)
        query_grad, key_part, value_part = attend_back(queries, grad_out, outputs, prompt_key, prompt_value, allowed, live_rows)
        return (state_now[0] + key_part, state_now[1] + value_part), query_grad

    shaped = lambda array: array.reshape(prompt_steps, prompt_block, H, DH)
    (prompt_kg, prompt_vg), prompt_qg = lax.scan(prompt_step, (zeros_prompt, zeros_prompt), (jnp.arange(prompt_steps), shaped(prompt_query), shaped(prompt_cotangent), shaped(prompt_output)))

    row_block = min(512, LENGTH)
    row_steps = LENGTH // row_block
    all_keys = PROMPT + LENGTH

    def response_step(state_now, inputs):
        queries, grad_out, outputs, own_keys, own_values, length = inputs
        key_rows = jnp.concatenate([prompt_key, own_keys], axis=0)
        value_rows = jnp.concatenate([prompt_value, own_values], axis=0)
        zeros_keys = jnp.zeros((all_keys, DH), jnp.float32)

        def block_step(inner, block_inputs):
            step_id, block_query, block_grad, block_out = block_inputs
            row_ids = step_id * row_block + jnp.arange(row_block)
            columns = jnp.arange(all_keys)
            allowed = (columns[None, :] < PROMPT) | ((columns - PROMPT)[None, :] <= row_ids[:, None])
            live_rows = (row_ids < length).astype(jnp.float32)

            def compute(operand):
                return attend_back(block_query, block_grad, block_out, key_rows, value_rows, allowed, live_rows)

            def skipped(operand):
                return jnp.zeros((row_block, H, DH), jnp.float32), zeros_keys, zeros_keys

            query_grad, key_part, value_part = lax.cond(length > step_id * row_block, compute, skipped, 0)
            return (inner[0] + key_part, inner[1] + value_part), query_grad

        reshape_rows = lambda array: array.reshape(row_steps, row_block, H, DH)
        (key_total, value_total), query_grad = lax.scan(block_step, (zeros_keys, zeros_keys), (jnp.arange(row_steps), reshape_rows(queries), reshape_rows(grad_out), reshape_rows(outputs)))
        new_state = (state_now[0] + key_total[:PROMPT], state_now[1] + value_total[:PROMPT])
        return new_state, (query_grad.reshape(LENGTH, H * DH), key_total[PROMPT:], value_total[PROMPT:])

    (shared_kg, shared_vg), (resp_qg, resp_kg, resp_vg) = lax.scan(response_step, (zeros_prompt, zeros_prompt), (response_query, response_cotangent, response_output, response_key, response_value, lengths))
    return (prompt_qg.reshape(PROMPT, H * DH).astype(jnp.bfloat16),
            (prompt_kg + shared_kg).astype(jnp.bfloat16),
            (prompt_vg + shared_vg).astype(jnp.bfloat16),
            resp_qg.astype(jnp.bfloat16),
            resp_kg.astype(jnp.bfloat16),
            resp_vg.astype(jnp.bfloat16))
```

```python
import functools

import jax
import jax.numpy as jnp
from jax import lax
from jax.experimental import pallas as pl
from jax.experimental.pallas import tpu as pltpu
from jax.sharding import PartitionSpec as P

f32 = jnp.float32
bf16 = jnp.bfloat16
LOG2E = 1.4426950408889634
MASKED = -1e30
NT = (((1,), (1,)), ((), ()))
NN = (((1,), (0,)), ((), ()))
TN = (((0,), (0,)), ((), ()))


def dot(a, b, dims):
    return lax.dot_general(a, b, dims, preferred_element_type=f32)


def kernel(
    NS, NC, H, KC, PR,
    pq_ref, pk_ref, pv_ref, pg_ref, po_ref, rq_ref, rk_ref, rv_ref, rg_ref, ro_ref, len_ref,
    dpq_ref, dpk_ref, dpv_ref, drq_ref, drk_ref, drv_ref,
    q, g, qp, gp, kall, vall, E, Ep, SA, SB, PB, GB, PBp, GBp,
    M2, S, Mj, Mt, Inv, D, M2p, Sp, Mjp, Dp, dqt, dqtp, DKV,
    keep, sibs, sibr, xs, xr, cs, cr, ownf, os_, or_,
    ks_s, ks_r, kf_s, kf_r, vs_s, vs_r, vf_s, vf_r, ok_s, ok_r, ov_s, ov_r,
    sib_s, sib_r, x_s, x_r, c_s, c_r, o_s, o_r,
):
    DH = 128
    RC = KC // 2
    NR = RC * H
    NPC = PR * H
    NP = NS // 2
    Y = NC // 2
    scaling = DH**-0.5
    C = scaling * LOG2E
    s_id = lax.axis_index("sample")
    c = lax.axis_index("ctx")
    core, zl, x = s_id % 2, (s_id // 2) % 2, s_id // 4
    zh, y = c % 2, c // 2
    pair = s_id // 2
    row0 = (s_id * NC + c) * PR
    jd = row0 // KC
    half = pl.ds(core * RC, RC)
    other = pl.ds((1 - core) * RC, RC)

    def dev(s, ct):
        return {"sample": s, "ctx": ct}

    sibling = dev(s_id + 1 - 2 * core, c)

    def rcopy(src, dst, send, recv, device):
        return pltpu.make_async_remote_copy(
            src_ref=src, dst_ref=dst, send_sem=send, recv_sem=recv,
            device_id=device, device_id_type=pl.DeviceIdType.MESH,
        )

    def g_dev(r):
        dy, dz = r // 2, r % 2
        zl2 = zl + dz - 2 * zl * dz
        zh2 = zh + dz - 2 * zh * dz
        return dev(x * 4 + zl2 * 2 + core, ((y + dy) % Y) * 2 + zh2)

    def g_src(r):
        dy, dz = r // 2, r % 2
        return ((y + Y - dy) % Y) * 2 + zh + dz - 2 * zh * dz

    def send_half(buf, ss, rs, r):
        return rcopy(buf.at[c, half], buf.at[c, half], ss.at[r], rs.at[r], g_dev(r))

    def got_half(buf, ss, rs, r):
        i = g_src(r)
        return rcopy(buf.at[i, half], buf.at[i, half], ss.at[r], rs.at[r], sibling)

    def got_other(buf, ss, rs, r):
        i = g_src(r)
        return rcopy(buf.at[i, other], buf.at[i, other], ss.at[r], rs.at[r], sibling)

    def own_at(buf, i):
        return buf.at[NC + i // 2, pl.ds((i % 2) * RC, RC)]

    def own_send(buf, ss, rs, to):
        return rcopy(own_at(buf, c), own_at(buf, c), ss.at[to], rs.at[c], dev(s_id, to))

    def own_got(buf, ss, rs, i):
        return rcopy(own_at(buf, i), own_at(buf, i), ss.at[i], rs.at[i], sibling)

    barrier = pltpu.get_barrier_semaphore()

    def greet(device):
        pl.semaphore_signal(
            barrier, inc=1, device_id=device, device_id_type=pl.DeviceIdType.MESH
        )

    greet(sibling)
    for t in range(1, NC):
        greet(dev(s_id, (c + t) % NC))
    for r in range(1, NC, 2):
        greet(g_dev(r))
    for t in range(1, NP):
        greet(dev(((pair + t) % NP) * 2 + core, c))

    kall[c] = pk_ref[...]
    vall[c] = pv_ref[...]
    kall[NC + c // 2, pl.ds((c % 2) * RC, RC)] = rk_ref[0]
    vall[NC + c // 2, pl.ds((c % 2) * RC, RC)] = rv_ref[0]

    @pl.when(c % 2 == 0)
    def _():
        kall[NC + c // 2, RC:] = jnp.zeros((RC, DH), bf16)
        vall[NC + c // 2, RC:] = jnp.zeros((RC, DH), bf16)

    pl.semaphore_wait(barrier, 1 + (NC - 1) + NC // 2 + (NP - 1))

    for r in range(1, NC):
        send_half(kall, ks_s, ks_r, r).start()

    @pl.loop(c + 1, NC)
    def _(to):
        own_send(kall, ok_s, ok_r, to).start()

    for r in range(1, NC):
        send_half(vall, vs_s, vs_r, r).start()

    @pl.loop(c + 1, NC)
    def _(to):
        own_send(vall, ov_s, ov_r, to).start()

    ones = jnp.ones((8, DH), bf16)

    def delta(gr, o):
        prod = gr.astype(f32) * o.astype(f32)
        hi = prod.astype(bf16)
        lo = (prod - hi.astype(f32)).astype(bf16)
        return dot(ones, hi, NT) + dot(ones, lo, NT)

    for h in range(H):
        cols = slice(h * DH, (h + 1) * DH)
        rows = slice(h * RC, (h + 1) * RC)
        q[rows] = rq_ref[0, :, cols]
        g[rows] = rg_ref[0, :, cols]
        qp[h * PR : (h + 1) * PR] = pq_ref[:, cols]
        gp[h * PR : (h + 1) * PR] = pg_ref[:, cols]
        D[:, rows] = delta(rg_ref[0, :, cols], ro_ref[0, :, cols])
    prod_o = jnp.concatenate([po_ref[:, h * DH : (h + 1) * DH] for h in range(H)], axis=0)
    Dp[...] = delta(gp[...], prod_o)
    M2[...] = jnp.full_like(M2, MASKED)
    S[...] = jnp.zeros_like(S)
    M2p[...] = jnp.full_like(M2p, MASKED)
    Sp[...] = jnp.zeros_like(Sp)
    dqt[...] = jnp.zeros_like(dqt)
    dqtp[...] = jnp.zeros_like(dqtp)

    L = NC + c // 2

    def id_of(p):
        own = p // NC
        return g_src(p % NC) * (1 - own) + p * own

    def first(i_id, buf, h):
        cols = slice(h * RC, (h + 1) * RC)
        s = dot(kall[i_id], q[cols], NT)
        buf[:, cols] = s
        M2[0, :, cols] = jnp.maximum(
            M2[0, :, cols], jnp.max(s.reshape(KC // 8, 8, RC), axis=0)
        )

    def second(i_id, buf, h):
        cols = slice(h * RC, (h + 1) * RC)
        s = buf[:, cols].reshape(KC // 8, 8, RC)
        new, old = M2[1, :, cols], M2[2, :, cols]
        e = jnp.exp2((s - new) * C)
        S[:, cols] = S[:, cols] * jnp.exp2((old - new) * C) + jnp.sum(e, axis=0)
        E[pl.ds(pl.multiple_of(i_id * KC, KC), KC), cols] = e.reshape(KC, RC).astype(bf16)

    def rotate(i_id):
        M2[2] = M2[1]
        M2[1] = M2[0]
        Mj[i_id] = M2[0]

    def forward_k(p):
        @pl.when(p < NC)
        def _():
            got_half(kall, ks_s, ks_r, p).wait_recv()
            i = g_src(p)
            rcopy(kall.at[i, half], kall.at[i, half], kf_s.at[p], kf_r.at[p], sibling).start()

    def ready(p):
        forward_k(p + 1)

        @pl.when(p < NC)
        def _():
            got_other(kall, kf_s, kf_r, p).wait_recv()

        @pl.when((p >= NC) & (p < L))
        def _():
            own_got(kall, ok_s, ok_r, 2 * (p - NC)).wait_recv()
            own_got(kall, ok_s, ok_r, 2 * (p - NC) + 1).wait_recv()

    for h in range(H):
        first(c, SA, h)
    rotate(c)
    forward_k(1)

    @pl.loop(0, (L + 1) // 2)
    def _(t):
        p = 2 * t
        ready(p + 1)
        a, b = id_of(p), id_of(jnp.minimum(p + 1, L - 1))
        for h in range(H):
            first(b, SB, h)
            second(a, SA, h)
        rotate(b)

        @pl.when(p + 1 < L)
        def _():
            ready(p + 2)
            d = id_of(jnp.minimum(p + 2, L - 1))
            for h in range(H):
                first(d, SA, h)
                second(b, SB, h)
            rotate(d)

    @pl.when(c % 2 == 1)
    def _():
        own_got(kall, ok_s, ok_r, c - 1).wait_recv()

    dg = NC + c // 2
    key_at = lax.broadcasted_iota(jnp.int32, (KC, RC), 0)
    row_at = lax.broadcasted_iota(jnp.int32, (KC, RC), 1) + (c % 2) * RC
    seen = key_at <= row_at
    for h in range(H):
        cols = slice(h * RC, (h + 1) * RC)
        s = jnp.where(seen, dot(kall[dg], q[cols], NT), MASKED).reshape(KC // 8, 8, RC)
        old = M2[1, :, cols]
        new = jnp.maximum(old, jnp.max(s, axis=0))
        e = jnp.exp2((s - new) * C)
        S[:, cols] = S[:, cols] * jnp.exp2((old - new) * C) + jnp.sum(e, axis=0)
        E[pl.ds(pl.multiple_of(dg * KC, KC), KC), cols] = e.reshape(KC, RC).astype(bf16)
        Mj[dg, :, cols] = new
        M2[0, :, cols] = new

    for r in range(1, NC):
        got_half(vall, vs_s, vs_r, r).wait_recv()
        i = g_src(r)
        rcopy(vall.at[i, half], vall.at[i, half], vf_s.at[r], vf_r.at[r], sibling).start()

    @pl.loop(0, jd + 1)
    def _(j):
        s = dot(kall[j], qp[...], NT)
        keys = j * KC + lax.broadcasted_iota(jnp.int32, (KC, NPC), 0)
        rows = row0 + lax.broadcasted_iota(jnp.int32, (KC, NPC), 1) % PR
        ok = (keys <= rows).reshape(KC // 8, 8, NPC)
        s = jnp.where(ok, s.reshape(KC // 8, 8, NPC), MASKED)
        old = M2p[...]
        new = jnp.maximum(old, jnp.max(s, axis=0))
        e = jnp.where(ok, jnp.exp2((s - new) * C), 0.0)
        Sp[...] = Sp[...] * jnp.exp2((old - new) * C) + jnp.sum(e, axis=0)
        Ep[pl.ds(pl.multiple_of(j * KC, KC), KC)] = e.reshape(KC, NPC).astype(bf16)
        Mjp[j] = new
        M2p[...] = new

    length = len_ref[0]
    live = (c * RC + lax.broadcasted_iota(jnp.int32, (1, NR), 1) % RC) < length
    m = M2[0]
    mt = jnp.max(m, axis=0, keepdims=True)
    st = jnp.sum(S[...] * jnp.exp2((m - mt) * C), axis=0, keepdims=True)
    Mt[...] = mt
    Inv[...] = jnp.where(live, 1.0 / st, 0.0)
    mp = M2p[...]
    mpt = jnp.max(mp, axis=0, keepdims=True)
    invp = 1.0 / jnp.sum(Sp[...] * jnp.exp2((mp - mpt) * C), axis=0, keepdims=True)

    def grads(i_id):
        base = pl.ds(pl.multiple_of(i_id * KC, KC), KC)
        for h in range(H):
            cols = slice(h * RC, (h + 1) * RC)
            dp = dot(vall[i_id], g[cols], NT)
            w = jnp.exp2((Mj[i_id, :, cols] - Mt[:, cols]) * C) * Inv[:, cols]
            p = (E[base, cols].astype(f32).reshape(KC // 8, 8, RC) * w).astype(bf16)
            p = p.reshape(KC, RC)
            PB[:, cols] = p
            GB[:, cols] = (dp - D[0:1, cols]).astype(bf16) * p
        DKV[1] = dot(PB[...], g[...], NN)
        DKV[0] = dot(GB[...], q[...], NN)
        for h in range(H):
            cols = slice(h * RC, (h + 1) * RC)
            dqt[h] += dot(kall[i_id], GB[:, cols], TN)

    def grads_prompt(j):
        base = pl.ds(pl.multiple_of(j * KC, KC), KC)
        dp = dot(vall[j], gp[...], NT)
        w = jnp.exp2((Mjp[j] - mpt) * C) * invp
        p = (Ep[base].astype(f32).reshape(KC // 8, 8, NPC) * w).astype(bf16).reshape(KC, NPC)
        ds = (dp - Dp[0:1]).astype(bf16) * p
        DKV[1] += dot(p, gp[...], NN)
        DKV[0] += dot(ds, qp[...], NN)
        dqtp[...] += dot(kall[j], ds, TN)

    @pl.loop(0, c)
    def _(i):
        own_got(vall, ov_s, ov_r, i).wait_recv()

    def own_grad_send(to):
        return rcopy(os_.at[to], or_.at[c], o_s.at[to], o_r.at[c], dev(s_id, to))

    @pl.loop(0, c // 2 + 1)
    def _(jo):
        grads(NC + jo)
        for hf in range(2):
            to = 2 * jo + hf
            part = DKV[:, hf * RC : (hf + 1) * RC]

            @pl.when(to == c)
            def _():
                ownf[...] = part

            @pl.when(to < c)
            def _():
                os_[to] = jnp.stack([part[0] * scaling, part[1]]).astype(bf16)
                own_grad_send(to).start()

    for r in range(1, NC):
        got_other(vall, vf_s, vf_r, r).wait_recv()

    def sib_copy(i):
        return rcopy(sibs.at[i], sibr.at[i], sib_s.at[i], sib_r.at[i], sibling)

    def x_send(i):
        to = ((pair + 1 + i) % NP) * 2 + core
        return rcopy(xs.at[i], xr.at[pair], x_s.at[i], x_r.at[pair], dev(to, c))

    @pl.loop(0, NP)
    def _(i):
        j = (pair + 1 + i) % NP
        grads(j)

        @pl.when(j <= jd)
        def _():
            grads_prompt(j)

        keep[i, 0] = DKV[0, half] * scaling
        keep[i, 1] = DKV[1, half]
        sibs[i, 0] = (DKV[0, other] * scaling).astype(bf16)
        sibs[i, 1] = DKV[1, other].astype(bf16)
        sib_copy(i).start()

        @pl.when(i >= 1)
        def _():
            sib_copy(i - 1).wait_recv()
            xs[i - 1] = (keep[i - 1] + sibr[i - 1].astype(f32)).astype(bf16)
            x_send(i - 1).start()

    for h in range(H):
        cols = slice(h * DH, (h + 1) * DH)
        drq_ref[0, :, cols] = (dqt[h].T * scaling).astype(bf16)
    dqp = (dqtp[...].T * scaling).astype(bf16)
    for h in range(H):
        dpq_ref[:, h * DH : (h + 1) * DH] = dqp[h * PR : (h + 1) * PR]

    sib_copy(NP - 1).wait_recv()
    total = keep[NP - 1] + sibr[NP - 1].astype(f32)
    for t in range(1, NP):
        k = (pair + t) % NP
        rcopy(xr.at[k], xr.at[k], x_s.at[t - 1], x_r.at[k], sibling).wait_recv()
        total = total + xr[k].astype(f32)
    keep[NP - 1] = total

    def c_send(t):
        to = (c + t) % NC
        return rcopy(cs.at[t], cr.at[c], c_s.at[t], c_r.at[c], dev(s_id, to))

    for t in range(1, NC):
        to = (c + t) % NC
        cs[t] = keep[NP - 1, :, pl.ds(to * PR, PR)].astype(bf16)
        c_send(t).start()

    ownf[0] = ownf[0] * scaling

    @pl.loop(c + 1, NC)
    def _(i):
        rcopy(or_.at[i], or_.at[i], o_s.at[i], o_r.at[i], sibling).wait_recv()
        ownf[...] += or_[i].astype(f32)

    drk_ref[0] = ownf[0].astype(bf16)
    drv_ref[0] = ownf[1].astype(bf16)

    total = keep[NP - 1, :, pl.ds(c * PR, PR)]
    for t in range(1, NC):
        k = (c + t) % NC
        rcopy(cr.at[k], cr.at[k], c_s.at[t], c_r.at[k], sibling).wait_recv()
        total = total + cr[k].astype(f32)
    dpk_ref[...] = total[0].astype(bf16)
    dpv_ref[...] = total[1].astype(bf16)

    for r in range(1, NC):
        send_half(kall, ks_s, ks_r, r).wait_send()
        send_half(vall, vs_s, vs_r, r).wait_send()
        got_half(kall, kf_s, kf_r, r).wait_send()
        got_half(vall, vf_s, vf_r, r).wait_send()
        c_send(r).wait_send()

    @pl.loop(c + 1, NC)
    def _(to):
        own_send(kall, ok_s, ok_r, to).wait_send()
        own_send(vall, ov_s, ov_r, to).wait_send()

    @pl.loop(0, c)
    def _(to):
        own_grad_send(to).wait_send()

    for i in range(NP):
        sib_copy(i).wait_send()
    for i in range(NP - 1):
        x_send(i).wait_send()


def on_device(NS, NC, *args):
    pq, pk = args[0], args[1]
    rq = args[5]
    DH = pk.shape[1]
    H = pq.shape[1] // DH
    KC, PR, RC = pk.shape[0], pq.shape[0], rq.shape[1]
    NR, NPC, NP, NK = RC * H, PR * H, NS // 2, NC + NC // 2
    vm = pltpu.VMEM
    dma = pltpu.SemaphoreType.DMA
    sds = jax.ShapeDtypeStruct
    scratch = [
        vm((NR, DH), bf16), vm((NR, DH), bf16), vm((NPC, DH), bf16), vm((NPC, DH), bf16),
        vm((NK, KC, DH), bf16), vm((NK, KC, DH), bf16),
        vm((NK * KC, NR), bf16), vm((NC * KC, NPC), bf16),
        vm((KC, NR), f32), vm((KC, NR), f32), vm((KC, NR), bf16), vm((KC, NR), bf16),
        vm((8, 128), bf16), vm((8, 128), bf16),
        vm((3, 8, NR), f32), vm((8, NR), f32), vm((NK, 8, NR), f32), vm((1, NR), f32),
        vm((1, NR), f32), vm((8, NR), f32),
        vm((8, NPC), f32), vm((8, NPC), f32), vm((NC, 8, NPC), f32), vm((8, NPC), f32),
        vm((H, DH, RC), f32), vm((DH, NPC), f32), vm((2, KC, DH), f32),
        vm((NP, 2, RC, DH), f32), vm((NP, 2, RC, DH), bf16), vm((NP, 2, RC, DH), bf16),
        vm((NP, 2, RC, DH), bf16), vm((NP, 2, RC, DH), bf16),
        vm((NC, 2, PR, DH), bf16), vm((NC, 2, PR, DH), bf16),
        vm((2, RC, DH), f32), vm((NC, 2, RC, DH), bf16), vm((NC, 2, RC, DH), bf16),
    ]
    scratch += [dma((NC,))] * 12 + [dma((NP,))] * 4 + [dma((NC,))] * 4
    vspec = pl.BlockSpec(memory_space=pltpu.VMEM)
    return pl.pallas_call(
        functools.partial(kernel, NS, NC, H, KC, PR),
        out_shape=(
            sds((PR, H * DH), bf16), sds((PR, DH), bf16), sds((PR, DH), bf16),
            sds((1, RC, H * DH), bf16), sds((1, RC, DH), bf16), sds((1, RC, DH), bf16),
        ),
        in_specs=[vspec] * 10 + [pl.BlockSpec(memory_space=pltpu.SMEM)],
        out_specs=[vspec] * 6,
        scratch_shapes=scratch,
        compiler_params=pltpu.CompilerParams(
            collective_id=0, has_side_effects=True, vmem_limit_bytes=62 * 2**20
        ),
    )(*args)


def solution(mesh):
    placed = (
        P(("sample", "ctx"), None),
        P("ctx", None),
        P("ctx", None),
        P(("sample", "ctx"), None),
        P(("sample", "ctx"), None),
        P("sample", "ctx", None),
        P("sample", "ctx", None),
        P("sample", "ctx", None),
        P("sample", "ctx", None),
        P("sample", "ctx", None),
        P("sample"),
    )
    return jax.shard_map(
        functools.partial(on_device, mesh.shape["sample"], mesh.shape["ctx"]),
        mesh=mesh,
        in_specs=placed,
        out_specs=(
            P(("sample", "ctx"), None),
            P(("sample", "ctx"), None),
            P(("sample", "ctx"), None),
            P("sample", "ctx", None),
            P("sample", "ctx", None),
            P("sample", "ctx", None),
        ),
        check_vma=False,
    )
```

```python
import functools

import jax
import jax.numpy as jnp
from jax import lax
from jax.experimental import pallas as pl
from jax.experimental.pallas import tpu as pltpu
from jax.sharding import PartitionSpec as P

f32 = jnp.float32
bf16 = jnp.bfloat16
LOG2E = 1.4426950408889634
MASKED = -1e30
NT = (((1,), (1,)), ((), ()))
NN = (((1,), (0,)), ((), ()))
TN = (((0,), (0,)), ((), ()))


def dot(a, b, dims):
    return lax.dot_general(a, b, dims, preferred_element_type=f32)


def kernel(
    NS, NC, H, KC, PR,
    pq_ref, pk_ref, pv_ref, pg_ref, po_ref, rq_ref, rk_ref, rv_ref, rg_ref, ro_ref, len_ref,
    dpq_ref, dpk_ref, dpv_ref, drq_ref, drk_ref, drv_ref,
    q, g, qp, gp, kall, vall, E, Ep, SA, SB, PB, GB, PBp, GBp,
    M2, S, Mj, Mt, Inv, D, M2p, Sp, Mjp, Dp, dqt, dqtp, DKV,
    keep, sibs, sibr, xs, xr, cs, cr, own_keep, os_, oy, oyr,
    ks_s, ks_r, kf_s, kf_r, vs_s, vs_r, ok_s, ok_r, oz_s, ov_s, ov_r, ow_s,
    vx_s, vx_r, vf_s, vf_r,
    sib_s, sib_r, x_s, x_r, c_s, c_r, o_s, o_r, oy_s, oy_r,
):
    DH = 128
    RC = KC // 2
    NR = RC * H
    NPC = PR * H
    NP = NS // 2
    X = NS // 4
    Y = NC // 2
    EW = KC // (2 * X)
    scaling = DH**-0.5
    C = scaling * LOG2E
    s_id = lax.axis_index("sample")
    c = lax.axis_index("ctx")
    core, zl, x = s_id % 2, (s_id // 2) % 2, s_id // 4
    zh, y = c % 2, c // 2
    pair = s_id // 2
    row0 = (s_id * NC + c) * PR
    jd = row0 // KC
    half = pl.ds(core * RC, RC)
    other = pl.ds((1 - core) * RC, RC)

    def dev(s, ct):
        return {"sample": s, "ctx": ct}

    sibling = dev(s_id + 1 - 2 * core, c)

    def rcopy(src, dst, send, recv, device):
        return pltpu.make_async_remote_copy(
            src_ref=src, dst_ref=dst, send_sem=send, recv_sem=recv,
            device_id=device, device_id_type=pl.DeviceIdType.MESH,
        )

    if Y == 4:
        places = ((0, 0), (0, 1), (1, 0), (3, 0), (1, 1), (2, 0), (2, 1), (3, 1))
    else:
        places = tuple((dy, dz) for dy in range(Y) for dz in range(2))

    def g_dev(p):
        dy, dz = places[p]
        zl2 = zl + dz - 2 * zl * dz
        zh2 = zh + dz - 2 * zh * dz
        return dev(x * 4 + zl2 * 2 + core, ((y + dy) % Y) * 2 + zh2)

    def r_of(j):
        dz = zh + j % 2 - 2 * zh * (j % 2)
        dy = (y + Y - j // 2) % Y
        off = dy * 2 + dz
        place = 0
        for p in range(1, NC):
            at = places[p][0] * 2 + places[p][1]
            differs = ((off + NC - at) % NC + NC - 1) // NC
            place = place + p * (1 - differs)
        return place

    def k_send(p):
        return rcopy(
            kall.at[0, half], kall.at[p, half], ks_s.at[p], ks_r.at[p], g_dev(p)
        )

    def k_hand(p):
        return rcopy(kall.at[p, half], kall.at[p, half], kf_s.at[p], kf_r.at[p], sibling)

    def e_send(buf, ss, rs, p):
        rows = pl.ds((x * 2 + core) * EW, EW)
        return rcopy(buf.at[0, rows], buf.at[p, rows], ss.at[p], rs.at[p], g_dev(p))

    def e_part(buf, lo, xi, ci):
        return buf.at[pl.ds(lo, NC - lo), pl.ds((xi * 2 + ci) * EW, EW)]

    def e_along(buf, lo, ss, rs, t):
        to = dev(((x + t) % X) * 4 + zl * 2 + core, c)
        part = e_part(buf, lo, x, core)
        return rcopy(part, part, ss.at[t], rs.at[t], to)

    def e_hand(buf, lo, ss, rs, t):
        part = e_part(buf, lo, (x + X - t) % X, core)
        return rcopy(part, part, ss.at[t], rs.at[t], sibling)

    def e_share(buf, lo, s1, r1, s2, r2, s3, r3):
        for p in range(lo, NC):
            e_send(buf, s1, r1, p).wait_recv()
        for t in range(1, X):
            e_along(buf, lo, s2, r2, t).start()
        e_hand(buf, lo, s3, r3, 0).start()

    def e_pass_on(buf, lo, s2, r2, s3, r3):
        for t in range(1, X):
            part = e_part(buf, lo, (x + X - t) % X, core)
            rcopy(part, part, s2.at[t], r2.at[t], sibling).wait_recv()
            e_hand(buf, lo, s3, r3, t).start()

    def e_arrive(buf, lo, s3, r3):
        for t in range(X):
            part = e_part(buf, lo, (x + X - t) % X, 1 - core)
            rcopy(part, part, s3.at[t], r3.at[t], sibling).wait_recv()

    def e_end(buf, lo, s1, r1, s2, r2, s3, r3):
        for p in range(lo, NC):
            e_send(buf, s1, r1, p).wait_send()
        for t in range(1, X):
            e_along(buf, lo, s2, r2, t).wait_send()
        for t in range(X):
            e_hand(buf, lo, s3, r3, t).wait_send()

    def own_at(buf, i):
        return buf.at[NC + i // 2, pl.ds((i % 2) * RC, RC)]

    def own_copy(buf, i, send, rs, to_y, to_zh):
        return rcopy(own_at(buf, i), own_at(buf, i), send, rs.at[i], dev(s_id, to_y * 2 + to_zh))

    def own_y(buf, ss, rs):
        return own_copy(buf, c, ss.at[0], rs, (y + 1) % Y, zh)

    def own_wrap(buf, ss, rs):
        return own_copy(buf, c, ss.at[1], rs, Y - 1, zh)

    def own_forward(buf, ss, rs):
        return own_copy(buf, c - 2, ss.at[2], rs, (y + 1) % Y, zh)

    def own_z(buf, zs, rs, yy):
        return own_copy(buf, yy * 2 + zh, zs.at[yy], rs, y, 1 - zh)

    def own_got(buf, rs, i):
        return rcopy(own_at(buf, i), own_at(buf, i), rs.at[i], rs.at[i], sibling)

    def own_start(buf, ss, zs, rs):
        @pl.when(y < Y - 1)
        def _():
            own_y(buf, ss, rs).start()

        if Y > 2:
            @pl.when(y == 0)
            def _():
                own_wrap(buf, ss, rs).start()

        @pl.when(zh == 0)
        def _():
            own_z(buf, zs, rs, y).start()

    def own_next(buf, ss, zs, rs):
        @pl.when(y >= 1)
        def _():
            own_got(buf, rs, c - 2).wait_recv()

            @pl.when(y < Y - 1)
            def _():
                own_forward(buf, ss, rs).start()

            own_z(buf, zs, rs, y - 1).start()

    def own_rest(buf, zs, rs):
        @pl.loop(0, jnp.maximum(y - 1, 0))
        def _(yy):
            own_got(buf, rs, yy * 2 + zh).wait_recv()
            own_z(buf, zs, rs, yy).start()

    def own_end(buf, ss, zs, rs):
        @pl.when(y < Y - 1)
        def _():
            own_y(buf, ss, rs).wait_send()

        if Y > 2:
            @pl.when(y == 0)
            def _():
                own_wrap(buf, ss, rs).wait_send()

        @pl.when((y >= 1) & (y < Y - 1))
        def _():
            own_forward(buf, ss, rs).wait_send()

        @pl.loop(0, y + 1 - zh)
        def _(yy):
            own_z(buf, zs, rs, yy).wait_send()

    barrier = pltpu.get_barrier_semaphore()

    def greet(device):
        pl.semaphore_signal(
            barrier, inc=1, device_id=device, device_id_type=pl.DeviceIdType.MESH
        )

    greet(sibling)
    for t in range(1, NC):
        greet(dev(s_id, (c + t) % NC))
    for p in range(1, NC):
        if places[p][1]:
            greet(g_dev(p))
    for t in range(1, NP):
        greet(dev(((pair + t) % NP) * 2 + core, c))

    kall[0] = pk_ref[...]
    vall[0] = pv_ref[...]
    kall[NC + c // 2, pl.ds((c % 2) * RC, RC)] = rk_ref[0]
    vall[NC + c // 2, pl.ds((c % 2) * RC, RC)] = rv_ref[0]

    @pl.when(c % 2 == 0)
    def _():
        kall[NC + c // 2, RC:] = jnp.zeros((RC, DH), bf16)
        vall[NC + c // 2, RC:] = jnp.zeros((RC, DH), bf16)

    pl.semaphore_wait(barrier, 1 + (NC - 1) + NC // 2 + (NP - 1))

    for p in range(1, NC):
        k_send(p).start()
    own_start(kall, ok_s, oz_s, ok_r)

    ones = jnp.ones((8, DH), bf16)

    def delta(gr, o):
        prod = gr.astype(f32) * o.astype(f32)
        hi = prod.astype(bf16)
        lo = (prod - hi.astype(f32)).astype(bf16)
        return dot(ones, hi, NT) + dot(ones, lo, NT)

    for h in range(H):
        cols = slice(h * DH, (h + 1) * DH)
        rows = slice(h * RC, (h + 1) * RC)
        q[rows] = rq_ref[0, :, cols]
        g[rows] = rg_ref[0, :, cols]
        qp[h * PR : (h + 1) * PR] = pq_ref[:, cols]
        gp[h * PR : (h + 1) * PR] = pg_ref[:, cols]
        D[:, rows] = delta(rg_ref[0, :, cols], ro_ref[0, :, cols])
    prod_o = jnp.concatenate([po_ref[:, h * DH : (h + 1) * DH] for h in range(H)], axis=0)
    Dp[...] = delta(gp[...], prod_o)
    M2[...] = jnp.full_like(M2, MASKED)
    S[...] = jnp.zeros_like(S)
    M2p[...] = jnp.full_like(M2p, MASKED)
    Sp[...] = jnp.zeros_like(Sp)
    dqt[...] = jnp.zeros_like(dqt)
    dqtp[...] = jnp.zeros_like(dqtp)

    def first(i_id, buf, h):
        cols = slice(h * RC, (h + 1) * RC)
        s = dot(kall[i_id], q[cols], NT)
        buf[:, cols] = s
        M2[0, :, cols] = jnp.maximum(
            M2[0, :, cols], jnp.max(s.reshape(KC // 8, 8, RC), axis=0)
        )

    def second(i_id, buf, h):
        cols = slice(h * RC, (h + 1) * RC)
        s = buf[:, cols].reshape(KC // 8, 8, RC)
        new, old = M2[1, :, cols], M2[2, :, cols]
        e = jnp.exp2((s - new) * C)
        S[:, cols] = S[:, cols] * jnp.exp2((old - new) * C) + jnp.sum(e, axis=0)
        E[pl.ds(pl.multiple_of(i_id * KC, KC), KC), cols] = e.reshape(KC, RC).astype(bf16)

    def rotate(i_id):
        M2[2] = M2[1]
        M2[1] = M2[0]
        Mj[i_id] = M2[0]

    values_e = (vall, 1, vs_s, vs_r, vx_s, vx_r, vf_s, vf_r)

    def hand(p):
        mine_ = kall.at[p, half]
        rcopy(mine_, mine_, ks_s.at[p], ks_r.at[p], sibling).wait_recv()
        k_hand(p).start()

    def handed(p):
        part = kall.at[p, other]
        rcopy(part, part, kf_s.at[p], kf_r.at[p], sibling).wait_recv()

    def step(a, b, bufa, bufb):
        for h in range(H):
            first(b, bufb, h)
            second(a, bufa, h)
        rotate(b)

    for h in range(H):
        first(0, SA, h)
    rotate(0)
    hand(1)

    @pl.loop(0, NC // 2 - 1)
    def _(t):
        p = 2 * t

        @pl.when(t == NC // 2 - 2)
        def _():
            own_next(kall, ok_s, oz_s, ok_r)
            for r in range(1, NC):
                e_send(vall, vs_s, vs_r, r).start()

        hand(p + 2)
        handed(p + 1)
        step(p, p + 1, SA, SB)
        hand(p + 3)
        handed(p + 2)
        step(p + 1, p + 2, SB, SA)

    own_rest(kall, oz_s, ok_r)
    handed(NC - 1)
    step(NC - 2, NC - 1, SA, SB)
    for h in range(H):
        second(NC - 1, SB, h)

    def own_weights(i_id, mask):
        for h in range(H):
            cols = slice(h * RC, (h + 1) * RC)
            s = dot(kall[i_id], q[cols], NT)
            if mask is not None:
                s = jnp.where(mask, s, MASKED)
            s = s.reshape(KC // 8, 8, RC)
            old = M2[0, :, cols]
            new = jnp.maximum(old, jnp.max(s, axis=0))
            e = jnp.exp2((s - new) * C)
            S[:, cols] = S[:, cols] * jnp.exp2((old - new) * C) + jnp.sum(e, axis=0)
            E[pl.ds(pl.multiple_of(i_id * KC, KC), KC), cols] = e.reshape(KC, RC).astype(bf16)
            Mj[i_id, :, cols] = new
            M2[0, :, cols] = new

    @pl.when(c % 2 == 1)
    def _():
        own_got(kall, ok_r, c - 1).wait_recv()

    dg = NC + y
    key_at = lax.broadcasted_iota(jnp.int32, (KC, RC), 0)
    row_at = lax.broadcasted_iota(jnp.int32, (KC, RC), 1) + zh * RC
    own_weights(dg, key_at <= row_at)
    e_share(*values_e)
    own_start(vall, ov_s, ow_s, ov_r)

    @pl.loop(0, y)
    def _(jo):
        own_got(kall, ok_r, 2 * jo + 1 - zh).wait_recv()
        own_weights(NC + jo, None)

    @pl.loop(0, jd + 1)
    def _(j):
        s = dot(kall[r_of(j)], qp[...], NT)
        keys = j * KC + lax.broadcasted_iota(jnp.int32, (KC, NPC), 0)
        rows = row0 + lax.broadcasted_iota(jnp.int32, (KC, NPC), 1) % PR
        ok = (keys <= rows).reshape(KC // 8, 8, NPC)
        s = jnp.where(ok, s.reshape(KC // 8, 8, NPC), MASKED)
        old = M2p[...]
        new = jnp.maximum(old, jnp.max(s, axis=0))
        e = jnp.where(ok, jnp.exp2((s - new) * C), 0.0)
        Sp[...] = Sp[...] * jnp.exp2((old - new) * C) + jnp.sum(e, axis=0)
        Ep[pl.ds(pl.multiple_of(j * KC, KC), KC)] = e.reshape(KC, NPC).astype(bf16)
        Mjp[j] = new
        M2p[...] = new

    e_pass_on(vall, 1, vx_s, vx_r, vf_s, vf_r)
    own_next(vall, ov_s, ow_s, ov_r)

    length = len_ref[0]
    live = (c * RC + lax.broadcasted_iota(jnp.int32, (1, NR), 1) % RC) < length
    m = M2[0]
    mt = jnp.max(m, axis=0, keepdims=True)
    st = jnp.sum(S[...] * jnp.exp2((m - mt) * C), axis=0, keepdims=True)
    Mt[...] = mt
    Inv[...] = jnp.where(live, 1.0 / st, 0.0)
    mp = M2p[...]
    mpt = jnp.max(mp, axis=0, keepdims=True)
    invp = 1.0 / jnp.sum(Sp[...] * jnp.exp2((mp - mpt) * C), axis=0, keepdims=True)

    def grads(i_id, between=None):
        base = pl.ds(pl.multiple_of(i_id * KC, KC), KC)
        for h in range(H):
            cols = slice(h * RC, (h + 1) * RC)
            dp = dot(vall[i_id], g[cols], NT)
            w = jnp.exp2((Mj[i_id, :, cols] - Mt[:, cols]) * C) * Inv[:, cols]
            p = (E[base, cols].astype(f32).reshape(KC // 8, 8, RC) * w).astype(bf16)
            p = p.reshape(KC, RC)
            PB[:, cols] = p
            GB[:, cols] = (dp - D[0:1, cols]).astype(bf16) * p
        if between is not None:
            between()
        DKV[1] = dot(PB[...], g[...], NN)
        DKV[0] = dot(GB[...], q[...], NN)
        for h in range(H):
            cols = slice(h * RC, (h + 1) * RC)
            dqt[h] += dot(kall[i_id], GB[:, cols], TN)

    def grads_prompt(j):
        base = pl.ds(pl.multiple_of(j * KC, KC), KC)
        r = r_of(j)
        dp = dot(vall[r], gp[...], NT)
        w = jnp.exp2((Mjp[j] - mpt) * C) * invp
        p = (Ep[base].astype(f32).reshape(KC // 8, 8, NPC) * w).astype(bf16).reshape(KC, NPC)
        ds = (dp - Dp[0:1]).astype(bf16) * p
        DKV[1] += dot(p, gp[...], NN)
        DKV[0] += dot(ds, qp[...], NN)
        dqtp[...] += dot(kall[r], ds, TN)

    e_arrive(vall, 1, vf_s, vf_r)

    def sib_copy(i):
        return rcopy(sibs.at[i], sibr.at[i], sib_s.at[i], sib_r.at[i], sibling)

    def x_send(i):
        to = ((pair + 1 + i) % NP) * 2 + core
        return rcopy(xs.at[i], xr.at[pair], x_s.at[i], x_r.at[pair], dev(to, c))

    mine = pl.ds(zh * RC, RC)
    theirs = pl.ds((1 - zh) * RC, RC)

    def oy_send(jo):
        return rcopy(oy.at[jo], oyr.at[y], oy_s.at[jo], oy_r.at[y], dev(s_id, jo * 2 + zh))

    def oz_send():
        return rcopy(
            os_.at[0], os_.at[1], o_s.at[0], o_r.at[0], dev(s_id, y * 2 + 1 - zh)
        )

    @pl.loop(0, NP)
    def _(i):
        j = (pair + 1 + i) % NP
        def pass_sum():
            @pl.when(i >= 1)
            def _():
                sib_copy(i - 1).wait_recv()
                xs[i - 1] = (keep[i - 1] + sibr[i - 1].astype(f32)).astype(bf16)
                x_send(i - 1).start()

        grads(r_of(j), pass_sum)

        @pl.when(j <= jd)
        def _():
            grads_prompt(j)

        @pl.when(i == 0)
        def _():
            own_rest(vall, ow_s, ov_r)

        keep[i, 0] = DKV[0, half] * scaling
        keep[i, 1] = DKV[1, half]
        sibs[i, 0] = (DKV[0, other] * scaling).astype(bf16)
        sibs[i, 1] = DKV[1, other].astype(bf16)
        sib_copy(i).start()

        @pl.when((i >= 2) & (i < y + 2))
        def _():
            jo = i - 2
            own_got(vall, ov_r, 2 * jo + 1 - zh).wait_recv()
            grads(NC + jo)
            oy[jo, 0] = (DKV[0] * scaling).astype(bf16)
            oy[jo, 1] = DKV[1].astype(bf16)
            oy_send(jo).start()

    def c_send(t):
        to = (c + t) % NC
        return rcopy(cs.at[t], cr.at[c], c_s.at[t], c_r.at[c], dev(s_id, to))

    def sum_prompt():
        sib_copy(NP - 1).wait_recv()
        total = keep[NP - 1] + sibr[NP - 1].astype(f32)
        for t in range(1, NP):
            k = (pair + t) % NP
            rcopy(xr.at[k], xr.at[k], x_s.at[t - 1], x_r.at[k], sibling).wait_recv()
            total = total + xr[k].astype(f32)
        keep[NP - 1] = total

        for t in range(1, NC):
            to = (c + t) % NC
            cs[t] = keep[NP - 1, :, pl.ds(to * PR, PR)].astype(bf16)
            c_send(t).start()

    @pl.when(zh == 1)
    def _():
        own_got(vall, ov_r, c - 1).wait_recv()

    grads(dg, sum_prompt)
    own_keep[0] = DKV[0] * scaling
    own_keep[1] = DKV[1]

    @pl.loop(y + 1, Y)
    def _(yy):
        rcopy(oyr.at[yy], oyr.at[yy], oy_s.at[yy], oy_r.at[yy], sibling).wait_recv()
        own_keep[...] += oyr[yy].astype(f32)

    os_[0] = own_keep[:, theirs].astype(bf16)
    oz_send().start()

    for h in range(H):
        cols = slice(h * DH, (h + 1) * DH)
        drq_ref[0, :, cols] = (dqt[h].T * scaling).astype(bf16)
    dqp = (dqtp[...].T * scaling).astype(bf16)
    for h in range(H):
        dpq_ref[:, h * DH : (h + 1) * DH] = dqp[h * PR : (h + 1) * PR]

    oz_send().wait_recv()
    total = own_keep[:, mine] + os_[1].astype(f32)
    drk_ref[0] = total[0].astype(bf16)
    drv_ref[0] = total[1].astype(bf16)

    total = keep[NP - 1, :, pl.ds(c * PR, PR)]
    for t in range(1, NC):
        k = (c + t) % NC
        rcopy(cr.at[k], cr.at[k], c_s.at[t], c_r.at[k], sibling).wait_recv()
        total = total + cr[k].astype(f32)
    dpk_ref[...] = total[0].astype(bf16)
    dpv_ref[...] = total[1].astype(bf16)

    for r in range(1, NC):
        c_send(r).wait_send()
    for p in range(1, NC):
        k_send(p).wait_send()
        k_hand(p).wait_send()
    e_end(*values_e)
    own_end(kall, ok_s, oz_s, ok_r)
    own_end(vall, ov_s, ow_s, ov_r)
    oz_send().wait_send()

    @pl.loop(0, y)
    def _(jo):
        oy_send(jo).wait_send()

    for i in range(NP):
        sib_copy(i).wait_send()
    for i in range(NP - 1):
        x_send(i).wait_send()


def copy_kernel(*refs):
    for i in range(6):
        refs[6 + i][...] = refs[i][...]


def on_device(NS, NC, *args):
    pq, pk = args[0], args[1]
    rq = args[5]
    DH = pk.shape[1]
    H = pq.shape[1] // DH
    KC, PR, RC = pk.shape[0], pq.shape[0], rq.shape[1]
    NR, NPC, NP, NK = RC * H, PR * H, NS // 2, NC + NC // 2
    vm = pltpu.VMEM
    dma = pltpu.SemaphoreType.DMA
    sds = jax.ShapeDtypeStruct
    scratch = [
        vm((NR, DH), bf16), vm((NR, DH), bf16), vm((NPC, DH), bf16), vm((NPC, DH), bf16),
        vm((NK, KC, DH), bf16), vm((NK, KC, DH), bf16),
        vm((NK * KC, NR), bf16), vm((NC * KC, NPC), bf16),
        vm((KC, NR), f32), vm((KC, NR), f32), vm((KC, NR), bf16), vm((KC, NR), bf16),
        vm((8, 128), bf16), vm((8, 128), bf16),
        vm((3, 8, NR), f32), vm((8, NR), f32), vm((NK, 8, NR), f32), vm((1, NR), f32),
        vm((1, NR), f32), vm((8, NR), f32),
        vm((8, NPC), f32), vm((8, NPC), f32), vm((NC, 8, NPC), f32), vm((8, NPC), f32),
        vm((H, DH, RC), f32), vm((DH, NPC), f32), vm((2, KC, DH), f32),
        vm((NP, 2, RC, DH), f32), vm((NP, 2, RC, DH), bf16), vm((NP, 2, RC, DH), bf16),
        vm((NP, 2, RC, DH), bf16), vm((NP, 2, RC, DH), bf16),
        vm((NC, 2, PR, DH), bf16), vm((NC, 2, PR, DH), bf16),
        vm((2, KC, DH), f32), vm((2, 2, RC, DH), bf16),
        vm((NC // 2, 2, KC, DH), bf16), vm((NC // 2, 2, KC, DH), bf16),
    ]
    scratch += [dma((NC,))] * 16 + [dma((NP,))] * 4 + [dma((NC,))] * 6
    vspec = pl.BlockSpec(memory_space=pltpu.VMEM)
    outs = pl.pallas_call(
        functools.partial(kernel, NS, NC, H, KC, PR),
        out_shape=(
            sds((PR, H * DH), bf16), sds((PR, DH), bf16), sds((PR, DH), bf16),
            sds((1, RC, H * DH), bf16), sds((1, RC, DH), bf16), sds((1, RC, DH), bf16),
        ),
        in_specs=[vspec] * 10 + [pl.BlockSpec(memory_space=pltpu.SMEM)],
        out_specs=[vspec] * 6,
        scratch_shapes=scratch,
        compiler_params=pltpu.CompilerParams(
            collective_id=0, has_side_effects=True, vmem_limit_bytes=62 * 2**20
        ),
    )(*args)
    return pl.pallas_call(
        copy_kernel,
        out_shape=tuple(sds(o.shape, o.dtype) for o in outs),
        in_specs=[vspec] * 6,
        out_specs=[vspec] * 6,
    )(*outs)


def solution(mesh):
    placed = (
        P(("sample", "ctx"), None),
        P("ctx", None),
        P("ctx", None),
        P(("sample", "ctx"), None),
        P(("sample", "ctx"), None),
        P("sample", "ctx", None),
        P("sample", "ctx", None),
        P("sample", "ctx", None),
        P("sample", "ctx", None),
        P("sample", "ctx", None),
        P("sample"),
    )
    return jax.shard_map(
        functools.partial(on_device, mesh.shape["sample"], mesh.shape["ctx"]),
        mesh=mesh,
        in_specs=placed,
        out_specs=(
            P(("sample", "ctx"), None),
            P(("sample", "ctx"), None),
            P(("sample", "ctx"), None),
            P("sample", "ctx", None),
            P("sample", "ctx", None),
            P("sample", "ctx", None),
        ),
        check_vma=False,
    )
```

```python
import functools

import jax
import jax.numpy as jnp
from jax import lax
from jax.experimental import pallas as pl
from jax.experimental.pallas import tpu as pltpu
from jax.sharding import PartitionSpec as P

f32 = jnp.float32
bf16 = jnp.bfloat16
LOG2E = 1.4426950408889634
MASKED = -1e30
NT = (((1,), (1,)), ((), ()))
NN = (((1,), (0,)), ((), ()))
TN = (((0,), (0,)), ((), ()))


def dot(a, b, dims):
    return lax.dot_general(a, b, dims, preferred_element_type=f32)


def kernel(
    NS, NC, H, KC, PR,
    pq_ref, pk_ref, pv_ref, pg_ref, po_ref, rq_ref, rk_ref, rv_ref, rg_ref, ro_ref, len_ref,
    dpq_ref, dpk_ref, dpv_ref, drq_ref, drk_ref, drv_ref,
    q, g, qp, gp, kall, vall, E, Ep, SA, SB, PB, GB, PBp, GBp,
    M2, S, Mj, Mt, Inv, D, M2p, Sp, Mjp, Dp, dqt, dqtp, DKV,
    keep, sibs, sibr, xs, xr, cs, cr, own_keep, os_, oy, oyr,
    ks_s, ks_r, kf_s, kf_r, vs_s, vs_r, ok_s, ok_r, oz_s, ov_s, ov_r, ow_s,
    vx_s, vx_r, vf_s, vf_r,
    sib_s, sib_r, x_s, x_r, c_s, c_r, o_s, o_r, oy_s, oy_r,
):
    DH = 128
    RC = KC // 2
    NR = RC * H
    NPC = PR * H
    NP = NS // 2
    X = NS // 4
    Y = NC // 2
    EW = KC // (2 * X)
    scaling = DH**-0.5
    C = scaling * LOG2E
    s_id = lax.axis_index("sample")
    c = lax.axis_index("ctx")
    core, zl, x = s_id % 2, (s_id // 2) % 2, s_id // 4
    zh, y = c % 2, c // 2
    pair = s_id // 2
    row0 = (s_id * NC + c) * PR
    jd = row0 // KC
    half = pl.ds(core * RC, RC)
    other = pl.ds((1 - core) * RC, RC)

    def dev(s, ct):
        return {"sample": s, "ctx": ct}

    sibling = dev(s_id + 1 - 2 * core, c)

    def rcopy(src, dst, send, recv, device):
        return pltpu.make_async_remote_copy(
            src_ref=src, dst_ref=dst, send_sem=send, recv_sem=recv,
            device_id=device, device_id_type=pl.DeviceIdType.MESH,
        )

    if Y == 4:
        places = ((0, 0), (0, 1), (1, 0), (3, 0), (1, 1), (2, 0), (2, 1), (3, 1))
    else:
        places = tuple((dy, dz) for dy in range(Y) for dz in range(2))

    def g_dev(p):
        dy, dz = places[p]
        zl2 = zl + dz - 2 * zl * dz
        zh2 = zh + dz - 2 * zh * dz
        return dev(x * 4 + zl2 * 2 + core, ((y + dy) % Y) * 2 + zh2)

    def r_of(j):
        dz = zh + j % 2 - 2 * zh * (j % 2)
        dy = (y + Y - j // 2) % Y
        off = dy * 2 + dz
        place = 0
        for p in range(1, NC):
            at = places[p][0] * 2 + places[p][1]
            differs = ((off + NC - at) % NC + NC - 1) // NC
            place = place + p * (1 - differs)
        return place

    def k_send(p):
        return rcopy(
            kall.at[0, half], kall.at[p, half], ks_s.at[p], ks_r.at[p], g_dev(p)
        )

    def k_hand(p):
        return rcopy(kall.at[p, half], kall.at[p, half], kf_s.at[p], kf_r.at[p], sibling)

    def e_send(buf, ss, rs, p):
        rows = pl.ds((x * 2 + core) * EW, EW)
        return rcopy(buf.at[0, rows], buf.at[p, rows], ss.at[p], rs.at[p], g_dev(p))

    def e_part(buf, lo, xi, ci):
        return buf.at[pl.ds(lo, NC - lo), pl.ds((xi * 2 + ci) * EW, EW)]

    def e_along(buf, lo, ss, rs, t):
        to = dev(((x + t) % X) * 4 + zl * 2 + core, c)
        part = e_part(buf, lo, x, core)
        return rcopy(part, part, ss.at[t], rs.at[t], to)

    def e_hand(buf, lo, ss, rs, t):
        part = e_part(buf, lo, (x + X - t) % X, core)
        return rcopy(part, part, ss.at[t], rs.at[t], sibling)

    def e_share(buf, lo, s1, r1, s2, r2, s3, r3):
        for p in range(lo, NC):
            e_send(buf, s1, r1, p).wait_recv()
        for t in range(1, X):
            e_along(buf, lo, s2, r2, t).start()
        e_hand(buf, lo, s3, r3, 0).start()

    def e_pass_on(buf, lo, s2, r2, s3, r3):
        for t in range(1, X):
            part = e_part(buf, lo, (x + X - t) % X, core)
            rcopy(part, part, s2.at[t], r2.at[t], sibling).wait_recv()
            e_hand(buf, lo, s3, r3, t).start()

    def e_arrive(buf, lo, s3, r3):
        for t in range(X):
            part = e_part(buf, lo, (x + X - t) % X, 1 - core)
            rcopy(part, part, s3.at[t], r3.at[t], sibling).wait_recv()

    def e_end(buf, lo, s1, r1, s2, r2, s3, r3):
        for p in range(lo, NC):
            e_send(buf, s1, r1, p).wait_send()
        for t in range(1, X):
            e_along(buf, lo, s2, r2, t).wait_send()
        for t in range(X):
            e_hand(buf, lo, s3, r3, t).wait_send()

    def own_at(buf, i):
        return buf.at[NC + i // 2, pl.ds((i % 2) * RC, RC)]

    def own_copy(buf, i, send, rs, to_y, to_zh):
        return rcopy(own_at(buf, i), own_at(buf, i), send, rs.at[i], dev(s_id, to_y * 2 + to_zh))

    def own_y(buf, ss, rs):
        return own_copy(buf, c, ss.at[0], rs, (y + 1) % Y, zh)

    def own_wrap(buf, ss, rs):
        return own_copy(buf, c, ss.at[1], rs, Y - 1, zh)

    def own_forward(buf, ss, rs):
        return own_copy(buf, c - 2, ss.at[2], rs, (y + 1) % Y, zh)

    def own_z(buf, zs, rs, yy):
        return own_copy(buf, yy * 2 + zh, zs.at[yy], rs, y, 1 - zh)

    def own_got(buf, rs, i):
        return rcopy(own_at(buf, i), own_at(buf, i), rs.at[i], rs.at[i], sibling)

    def own_start(buf, ss, zs, rs):
        @pl.when(y < Y - 1)
        def _():
            own_y(buf, ss, rs).start()

        if Y > 2:
            @pl.when(y == 0)
            def _():
                own_wrap(buf, ss, rs).start()

        @pl.when(zh == 0)
        def _():
            own_z(buf, zs, rs, y).start()

    def own_next(buf, ss, zs, rs):
        @pl.when(y >= 1)
        def _():
            own_got(buf, rs, c - 2).wait_recv()

            @pl.when(y < Y - 1)
            def _():
                own_forward(buf, ss, rs).start()

            own_z(buf, zs, rs, y - 1).start()

    def own_rest(buf, zs, rs):
        @pl.loop(0, jnp.maximum(y - 1, 0))
        def _(yy):
            own_got(buf, rs, yy * 2 + zh).wait_recv()
            own_z(buf, zs, rs, yy).start()

    def own_end(buf, ss, zs, rs):
        @pl.when(y < Y - 1)
        def _():
            own_y(buf, ss, rs).wait_send()

        if Y > 2:
            @pl.when(y == 0)
            def _():
                own_wrap(buf, ss, rs).wait_send()

        @pl.when((y >= 1) & (y < Y - 1))
        def _():
            own_forward(buf, ss, rs).wait_send()

        @pl.loop(0, y + 1 - zh)
        def _(yy):
            own_z(buf, zs, rs, yy).wait_send()

    barrier = pltpu.get_barrier_semaphore()

    def greet(device):
        pl.semaphore_signal(
            barrier, inc=1, device_id=device, device_id_type=pl.DeviceIdType.MESH
        )

    greet(sibling)
    for t in range(1, NC):
        greet(dev(s_id, (c + t) % NC))
    for p in range(1, NC):
        if places[p][1]:
            greet(g_dev(p))
    for t in range(1, NP):
        greet(dev(((pair + t) % NP) * 2 + core, c))

    kall[0] = pk_ref[...]
    vall[0] = pv_ref[...]
    kall[NC + c // 2, pl.ds((c % 2) * RC, RC)] = rk_ref[0]
    vall[NC + c // 2, pl.ds((c % 2) * RC, RC)] = rv_ref[0]

    @pl.when(c % 2 == 0)
    def _():
        kall[NC + c // 2, RC:] = jnp.zeros((RC, DH), bf16)
        vall[NC + c // 2, RC:] = jnp.zeros((RC, DH), bf16)

    pl.semaphore_wait(barrier, 1 + (NC - 1) + NC // 2 + (NP - 1))

    for p in range(1, NC // 2):
        k_send(p).start()
    own_start(kall, ok_s, oz_s, ok_r)
    for p in range(NC // 2, NC):
        k_send(p).start()

    ones = jnp.ones((8, DH), bf16)

    def delta(gr, o):
        prod = gr.astype(f32) * o.astype(f32)
        hi = prod.astype(bf16)
        lo = (prod - hi.astype(f32)).astype(bf16)
        return dot(ones, hi, NT) + dot(ones, lo, NT)

    for h in range(H):
        cols = slice(h * DH, (h + 1) * DH)
        rows = slice(h * RC, (h + 1) * RC)
        q[rows] = rq_ref[0, :, cols]
        g[rows] = rg_ref[0, :, cols]
        qp[h * PR : (h + 1) * PR] = pq_ref[:, cols]
        gp[h * PR : (h + 1) * PR] = pg_ref[:, cols]
        D[:, rows] = delta(rg_ref[0, :, cols], ro_ref[0, :, cols])
    prod_o = jnp.concatenate([po_ref[:, h * DH : (h + 1) * DH] for h in range(H)], axis=0)
    Dp[...] = delta(gp[...], prod_o)
    M2[...] = jnp.full_like(M2, MASKED)
    S[...] = jnp.zeros_like(S)
    M2p[...] = jnp.full_like(M2p, MASKED)
    Sp[...] = jnp.zeros_like(Sp)
    dqt[...] = jnp.zeros_like(dqt)
    dqtp[...] = jnp.zeros_like(dqtp)

    def first(i_id, buf, h):
        cols = slice(h * RC, (h + 1) * RC)
        s = dot(kall[i_id], q[cols], NT)
        buf[:, cols] = s
        M2[0, :, cols] = jnp.maximum(
            M2[0, :, cols], jnp.max(s.reshape(KC // 8, 8, RC), axis=0)
        )

    def second(i_id, buf, h):
        cols = slice(h * RC, (h + 1) * RC)
        s = buf[:, cols].reshape(KC // 8, 8, RC)
        new, old = M2[1, :, cols], M2[2, :, cols]
        e = jnp.exp2((s - new) * C)
        S[:, cols] = S[:, cols] * jnp.exp2((old - new) * C) + jnp.sum(e, axis=0)
        E[pl.ds(pl.multiple_of(i_id * KC, KC), KC), cols] = e.reshape(KC, RC).astype(bf16)

    def rotate(i_id):
        M2[2] = M2[1]
        M2[1] = M2[0]
        Mj[i_id] = M2[0]

    values_e = (vall, 1, vs_s, vs_r, vx_s, vx_r, vf_s, vf_r)

    def hand(p):
        mine_ = kall.at[p, half]
        rcopy(mine_, mine_, ks_s.at[p], ks_r.at[p], sibling).wait_recv()
        k_hand(p).start()

    def handed(p):
        part = kall.at[p, other]
        rcopy(part, part, kf_s.at[p], kf_r.at[p], sibling).wait_recv()

    def step(a, b, bufa, bufb):
        for h in range(H):
            first(b, bufb, h)
            second(a, bufa, h)
        rotate(b)

    for h in range(H):
        first(0, SA, h)
    rotate(0)
    hand(1)

    @pl.loop(0, NC // 2 - 1)
    def _(t):
        p = 2 * t

        @pl.when(t == NC // 2 - 2)
        def _():
            own_next(kall, ok_s, oz_s, ok_r)
            for r in range(1, NC):
                e_send(vall, vs_s, vs_r, r).start()

        hand(p + 2)
        handed(p + 1)
        step(p, p + 1, SA, SB)
        hand(p + 3)
        handed(p + 2)
        step(p + 1, p + 2, SB, SA)

    own_rest(kall, oz_s, ok_r)
    handed(NC - 1)
    step(NC - 2, NC - 1, SA, SB)
    for h in range(H):
        second(NC - 1, SB, h)

    def own_weights(i_id, mask):
        for h in range(H):
            cols = slice(h * RC, (h + 1) * RC)
            s = dot(kall[i_id], q[cols], NT)
            if mask is not None:
                s = jnp.where(mask, s, MASKED)
            s = s.reshape(KC // 8, 8, RC)
            old = M2[0, :, cols]
            new = jnp.maximum(old, jnp.max(s, axis=0))
            e = jnp.exp2((s - new) * C)
            S[:, cols] = S[:, cols] * jnp.exp2((old - new) * C) + jnp.sum(e, axis=0)
            E[pl.ds(pl.multiple_of(i_id * KC, KC), KC), cols] = e.reshape(KC, RC).astype(bf16)
            Mj[i_id, :, cols] = new
            M2[0, :, cols] = new

    @pl.when(c % 2 == 1)
    def _():
        own_got(kall, ok_r, c - 1).wait_recv()

    dg = NC + y
    key_at = lax.broadcasted_iota(jnp.int32, (KC, RC), 0)
    row_at = lax.broadcasted_iota(jnp.int32, (KC, RC), 1) + zh * RC
    own_weights(dg, key_at <= row_at)
    e_share(*values_e)
    own_start(vall, ov_s, ow_s, ov_r)

    @pl.loop(0, jd + 1)
    def _(j):
        s = dot(kall[r_of(j)], qp[...], NT)
        keys = j * KC + lax.broadcasted_iota(jnp.int32, (KC, NPC), 0)
        rows = row0 + lax.broadcasted_iota(jnp.int32, (KC, NPC), 1) % PR
        ok = (keys <= rows).reshape(KC // 8, 8, NPC)
        s = jnp.where(ok, s.reshape(KC // 8, 8, NPC), MASKED)
        old = M2p[...]
        new = jnp.maximum(old, jnp.max(s, axis=0))
        e = jnp.where(ok, jnp.exp2((s - new) * C), 0.0)
        Sp[...] = Sp[...] * jnp.exp2((old - new) * C) + jnp.sum(e, axis=0)
        Ep[pl.ds(pl.multiple_of(j * KC, KC), KC)] = e.reshape(KC, NPC).astype(bf16)
        Mjp[j] = new
        M2p[...] = new

    @pl.loop(0, y)
    def _(jo):
        own_got(kall, ok_r, 2 * jo + 1 - zh).wait_recv()
        own_weights(NC + jo, None)

    e_pass_on(vall, 1, vx_s, vx_r, vf_s, vf_r)
    own_next(vall, ov_s, ow_s, ov_r)

    length = len_ref[0]
    live = (c * RC + lax.broadcasted_iota(jnp.int32, (1, NR), 1) % RC) < length
    m = M2[0]
    mt = jnp.max(m, axis=0, keepdims=True)
    st = jnp.sum(S[...] * jnp.exp2((m - mt) * C), axis=0, keepdims=True)
    Mt[...] = mt
    Inv[...] = jnp.where(live, 1.0 / st, 0.0)
    mp = M2p[...]
    mpt = jnp.max(mp, axis=0, keepdims=True)
    invp = 1.0 / jnp.sum(Sp[...] * jnp.exp2((mp - mpt) * C), axis=0, keepdims=True)

    def grads(i_id, between=None):
        base = pl.ds(pl.multiple_of(i_id * KC, KC), KC)
        for h in range(H):
            cols = slice(h * RC, (h + 1) * RC)
            dp = dot(vall[i_id], g[cols], NT)
            w = jnp.exp2((Mj[i_id, :, cols] - Mt[:, cols]) * C) * Inv[:, cols]
            p = (E[base, cols].astype(f32).reshape(KC // 8, 8, RC) * w).astype(bf16)
            p = p.reshape(KC, RC)
            PB[:, cols] = p
            GB[:, cols] = (dp - D[0:1, cols]).astype(bf16) * p
        if between is not None:
            between()
        DKV[1] = dot(PB[...], g[...], NN)
        DKV[0] = dot(GB[...], q[...], NN)
        for h in range(H):
            cols = slice(h * RC, (h + 1) * RC)
            dqt[h] += dot(kall[i_id], GB[:, cols], TN)

    def grads_prompt(j):
        base = pl.ds(pl.multiple_of(j * KC, KC), KC)
        r = r_of(j)
        dp = dot(vall[r], gp[...], NT)
        w = jnp.exp2((Mjp[j] - mpt) * C) * invp
        p = (Ep[base].astype(f32).reshape(KC // 8, 8, NPC) * w).astype(bf16).reshape(KC, NPC)
        ds = (dp - Dp[0:1]).astype(bf16) * p
        DKV[1] += dot(p, gp[...], NN)
        DKV[0] += dot(ds, qp[...], NN)
        dqtp[...] += dot(kall[r], ds, TN)

    e_arrive(vall, 1, vf_s, vf_r)

    def sib_copy(i):
        return rcopy(sibs.at[i], sibr.at[i], sib_s.at[i], sib_r.at[i], sibling)

    def x_send(i):
        to = ((pair + 1 + i) % NP) * 2 + core
        return rcopy(xs.at[i], xr.at[pair], x_s.at[i], x_r.at[pair], dev(to, c))

    mine = pl.ds(zh * RC, RC)
    theirs = pl.ds((1 - zh) * RC, RC)

    def oy_send(jo):
        return rcopy(oy.at[jo], oyr.at[y], oy_s.at[jo], oy_r.at[y], dev(s_id, jo * 2 + zh))

    def oz_send():
        return rcopy(
            os_.at[0], os_.at[1], o_s.at[0], o_r.at[0], dev(s_id, y * 2 + 1 - zh)
        )

    @pl.loop(0, NP)
    def _(i):
        j = (pair + 1 + i) % NP
        grads(r_of(j))

        @pl.when(j <= jd)
        def _():
            grads_prompt(j)

        @pl.when(i == 0)
        def _():
            own_rest(vall, ow_s, ov_r)

        keep[i, 0] = DKV[0, half] * scaling
        keep[i, 1] = DKV[1, half]
        sibs[i, 0] = (DKV[0, other] * scaling).astype(bf16)
        sibs[i, 1] = DKV[1, other].astype(bf16)
        sib_copy(i).start()

        @pl.when(i >= 1)
        def _():
            sib_copy(i - 1).wait_recv()
            xs[i - 1] = (keep[i - 1] + sibr[i - 1].astype(f32)).astype(bf16)
            x_send(i - 1).start()

        @pl.when((i >= 2) & (i < y + 2))
        def _():
            jo = i - 2
            own_got(vall, ov_r, 2 * jo + 1 - zh).wait_recv()
            grads(NC + jo)
            oy[jo, 0] = (DKV[0] * scaling).astype(bf16)
            oy[jo, 1] = DKV[1].astype(bf16)
            oy_send(jo).start()

    def c_send(t):
        to = (c + t) % NC
        return rcopy(cs.at[t], cr.at[c], c_s.at[t], c_r.at[c], dev(s_id, to))

    def sum_prompt():
        sib_copy(NP - 1).wait_recv()
        total = keep[NP - 1] + sibr[NP - 1].astype(f32)
        for t in range(1, NP):
            k = (pair + t) % NP
            rcopy(xr.at[k], xr.at[k], x_s.at[t - 1], x_r.at[k], sibling).wait_recv()
            total = total + xr[k].astype(f32)
        keep[NP - 1] = total

        for t in range(1, NC):
            to = (c + t) % NC
            cs[t] = keep[NP - 1, :, pl.ds(to * PR, PR)].astype(bf16)
            c_send(t).start()

    @pl.when(zh == 1)
    def _():
        own_got(vall, ov_r, c - 1).wait_recv()

    grads(dg, sum_prompt)
    own_keep[0] = DKV[0] * scaling
    own_keep[1] = DKV[1]

    @pl.loop(y + 1, Y)
    def _(yy):
        rcopy(oyr.at[yy], oyr.at[yy], oy_s.at[yy], oy_r.at[yy], sibling).wait_recv()
        own_keep[...] += oyr[yy].astype(f32)

    os_[0] = own_keep[:, theirs].astype(bf16)
    oz_send().start()

    for h in range(H):
        cols = slice(h * DH, (h + 1) * DH)
        drq_ref[0, :, cols] = (dqt[h].T * scaling).astype(bf16)
    dqp = (dqtp[...].T * scaling).astype(bf16)
    for h in range(H):
        dpq_ref[:, h * DH : (h + 1) * DH] = dqp[h * PR : (h + 1) * PR]

    oz_send().wait_recv()
    total = own_keep[:, mine] + os_[1].astype(f32)
    drk_ref[0] = total[0].astype(bf16)
    drv_ref[0] = total[1].astype(bf16)

    total = keep[NP - 1, :, pl.ds(c * PR, PR)]
    for t in range(1, NC):
        k = (c + t) % NC
        rcopy(cr.at[k], cr.at[k], c_s.at[t], c_r.at[k], sibling).wait_recv()
        total = total + cr[k].astype(f32)
    dpk_ref[...] = total[0].astype(bf16)
    dpv_ref[...] = total[1].astype(bf16)

    for r in range(1, NC):
        c_send(r).wait_send()
    for p in range(1, NC):
        k_send(p).wait_send()
        k_hand(p).wait_send()
    e_end(*values_e)
    own_end(kall, ok_s, oz_s, ok_r)
    own_end(vall, ov_s, ow_s, ov_r)
    oz_send().wait_send()

    @pl.loop(0, y)
    def _(jo):
        oy_send(jo).wait_send()

    for i in range(NP):
        sib_copy(i).wait_send()
    for i in range(NP - 1):
        x_send(i).wait_send()


def copy_kernel(*refs):
    for i in range(6):
        refs[6 + i][...] = refs[i][...]


def on_device(NS, NC, *args):
    pq, pk = args[0], args[1]
    rq = args[5]
    DH = pk.shape[1]
    H = pq.shape[1] // DH
    KC, PR, RC = pk.shape[0], pq.shape[0], rq.shape[1]
    NR, NPC, NP, NK = RC * H, PR * H, NS // 2, NC + NC // 2
    vm = pltpu.VMEM
    dma = pltpu.SemaphoreType.DMA
    sds = jax.ShapeDtypeStruct
    scratch = [
        vm((NR, DH), bf16), vm((NR, DH), bf16), vm((NPC, DH), bf16), vm((NPC, DH), bf16),
        vm((NK, KC, DH), bf16), vm((NK, KC, DH), bf16),
        vm((NK * KC, NR), bf16), vm((NC * KC, NPC), bf16),
        vm((KC, NR), f32), vm((KC, NR), f32), vm((KC, NR), bf16), vm((KC, NR), bf16),
        vm((8, 128), bf16), vm((8, 128), bf16),
        vm((3, 8, NR), f32), vm((8, NR), f32), vm((NK, 8, NR), f32), vm((1, NR), f32),
        vm((1, NR), f32), vm((8, NR), f32),
        vm((8, NPC), f32), vm((8, NPC), f32), vm((NC, 8, NPC), f32), vm((8, NPC), f32),
        vm((H, DH, RC), f32), vm((DH, NPC), f32), vm((2, KC, DH), f32),
        vm((NP, 2, RC, DH), f32), vm((NP, 2, RC, DH), bf16), vm((NP, 2, RC, DH), bf16),
        vm((NP, 2, RC, DH), bf16), vm((NP, 2, RC, DH), bf16),
        vm((NC, 2, PR, DH), bf16), vm((NC, 2, PR, DH), bf16),
        vm((2, KC, DH), f32), vm((2, 2, RC, DH), bf16),
        vm((NC // 2, 2, KC, DH), bf16), vm((NC // 2, 2, KC, DH), bf16),
    ]
    scratch += [dma((NC,))] * 16 + [dma((NP,))] * 4 + [dma((NC,))] * 6
    vspec = pl.BlockSpec(memory_space=pltpu.VMEM)
    outs = pl.pallas_call(
        functools.partial(kernel, NS, NC, H, KC, PR),
        out_shape=(
            sds((PR, H * DH), bf16), sds((PR, DH), bf16), sds((PR, DH), bf16),
            sds((1, RC, H * DH), bf16), sds((1, RC, DH), bf16), sds((1, RC, DH), bf16),
        ),
        in_specs=[vspec] * 10 + [pl.BlockSpec(memory_space=pltpu.SMEM)],
        out_specs=[vspec] * 6,
        scratch_shapes=scratch,
        compiler_params=pltpu.CompilerParams(
            collective_id=0, has_side_effects=True, vmem_limit_bytes=62 * 2**20
        ),
    )(*args)
    return pl.pallas_call(
        copy_kernel,
        out_shape=tuple(sds(o.shape, o.dtype) for o in outs),
        in_specs=[vspec] * 6,
        out_specs=[vspec] * 6,
    )(*outs)


def solution(mesh):
    placed = (
        P(("sample", "ctx"), None),
        P("ctx", None),
        P("ctx", None),
        P(("sample", "ctx"), None),
        P(("sample", "ctx"), None),
        P("sample", "ctx", None),
        P("sample", "ctx", None),
        P("sample", "ctx", None),
        P("sample", "ctx", None),
        P("sample", "ctx", None),
        P("sample"),
    )
    return jax.shard_map(
        functools.partial(on_device, mesh.shape["sample"], mesh.shape["ctx"]),
        mesh=mesh,
        in_specs=placed,
        out_specs=(
            P(("sample", "ctx"), None),
            P(("sample", "ctx"), None),
            P(("sample", "ctx"), None),
            P("sample", "ctx", None),
            P("sample", "ctx", None),
            P("sample", "ctx", None),
        ),
        check_vma=False,
    )
```

```python
import functools

import jax
import jax.numpy as jnp
from jax import lax
from jax.experimental import pallas as pl
from jax.experimental.pallas import tpu as pltpu
from jax.sharding import PartitionSpec as P

f32 = jnp.float32
bf16 = jnp.bfloat16
LOG2E = 1.4426950408889634
MASKED = -1e30
NT = (((1,), (1,)), ((), ()))
NN = (((1,), (0,)), ((), ()))
TN = (((0,), (0,)), ((), ()))


def dot(a, b, dims):
    return lax.dot_general(a, b, dims, preferred_element_type=f32)


def kernel(
    NS, NC, H, KC, PR,
    pq_ref, pk_ref, pv_ref, pg_ref, po_ref, rq_ref, rk_ref, rv_ref, rg_ref, ro_ref, len_ref,
    dpq_ref, dpk_ref, dpv_ref, drq_ref, drk_ref, drv_ref,
    q, g, qp, gp, kall, vall, E, Ep, SA, SB, PB, GB, PBp, GBp,
    M2, S, Mj, Mt, Inv, D, M2p, Sp, Mjp, Dp, dqt, dqtp, DKV,
    keep, sibs, sibr, xs, xr, cs, cr, own_keep, os_, oy, oyr,
    ks_s, ks_r, kf_s, kf_r, vs_s, vs_r, ok_s, ok_r, oz_s, ov_s, ov_r, ow_s,
    vx_s, vx_r, vf_s, vf_r,
    sib_s, sib_r, x_s, x_r, c_s, c_r, o_s, o_r, oy_s, oy_r,
):
    DH = 128
    RC = KC // 2
    NR = RC * H
    NPC = PR * H
    NP = NS // 2
    X = NS // 4
    Y = NC // 2
    EW = KC // (2 * X)
    scaling = DH**-0.5
    C = scaling * LOG2E
    s_id = lax.axis_index("sample")
    c = lax.axis_index("ctx")
    core, zl, x = s_id % 2, (s_id // 2) % 2, s_id // 4
    zh, y = c % 2, c // 2
    pair = s_id // 2
    row0 = (s_id * NC + c) * PR
    jd = row0 // KC
    half = pl.ds(core * RC, RC)
    other = pl.ds((1 - core) * RC, RC)

    def dev(s, ct):
        return {"sample": s, "ctx": ct}

    sibling = dev(s_id + 1 - 2 * core, c)

    def rcopy(src, dst, send, recv, device):
        return pltpu.make_async_remote_copy(
            src_ref=src, dst_ref=dst, send_sem=send, recv_sem=recv,
            device_id=device, device_id_type=pl.DeviceIdType.MESH,
        )

    if Y == 4:
        places = ((0, 0), (0, 1), (1, 0), (3, 0), (1, 1), (2, 0), (2, 1), (3, 1))
    else:
        places = tuple((dy, dz) for dy in range(Y) for dz in range(2))

    def g_dev(p):
        dy, dz = places[p]
        zl2 = zl + dz - 2 * zl * dz
        zh2 = zh + dz - 2 * zh * dz
        return dev(x * 4 + zl2 * 2 + core, ((y + dy) % Y) * 2 + zh2)

    def r_of(j):
        dz = zh + j % 2 - 2 * zh * (j % 2)
        dy = (y + Y - j // 2) % Y
        off = dy * 2 + dz
        place = 0
        for p in range(1, NC):
            at = places[p][0] * 2 + places[p][1]
            differs = ((off + NC - at) % NC + NC - 1) // NC
            place = place + p * (1 - differs)
        return place

    def k_send(p):
        return rcopy(
            kall.at[0, half], kall.at[p, half], ks_s.at[p], ks_r.at[p], g_dev(p)
        )

    def k_hand(p):
        return rcopy(kall.at[p, half], kall.at[p, half], kf_s.at[p], kf_r.at[p], sibling)

    def e_send(buf, ss, rs, p):
        rows = pl.ds((x * 2 + core) * EW, EW)
        return rcopy(buf.at[0, rows], buf.at[p, rows], ss.at[p], rs.at[p], g_dev(p))

    def e_part(buf, lo, xi, ci):
        return buf.at[pl.ds(lo, NC - lo), pl.ds((xi * 2 + ci) * EW, EW)]

    def e_along(buf, lo, ss, rs, t):
        to = dev(((x + t) % X) * 4 + zl * 2 + core, c)
        part = e_part(buf, lo, x, core)
        return rcopy(part, part, ss.at[t], rs.at[t], to)

    def e_hand(buf, lo, ss, rs, t):
        part = e_part(buf, lo, (x + X - t) % X, core)
        return rcopy(part, part, ss.at[t], rs.at[t], sibling)

    def e_share(buf, lo, s1, r1, s2, r2, s3, r3):
        for p in range(lo, NC):
            e_send(buf, s1, r1, p).wait_recv()
        for t in range(1, X):
            e_along(buf, lo, s2, r2, t).start()
        e_hand(buf, lo, s3, r3, 0).start()

    def e_pass_on(buf, lo, s2, r2, s3, r3):
        for t in range(1, X):
            part = e_part(buf, lo, (x + X - t) % X, core)
            rcopy(part, part, s2.at[t], r2.at[t], sibling).wait_recv()
            e_hand(buf, lo, s3, r3, t).start()

    def e_arrive(buf, lo, s3, r3):
        for t in range(X):
            part = e_part(buf, lo, (x + X - t) % X, 1 - core)
            rcopy(part, part, s3.at[t], r3.at[t], sibling).wait_recv()

    def e_end(buf, lo, s1, r1, s2, r2, s3, r3):
        for p in range(lo, NC):
            e_send(buf, s1, r1, p).wait_send()
        for t in range(1, X):
            e_along(buf, lo, s2, r2, t).wait_send()
        for t in range(X):
            e_hand(buf, lo, s3, r3, t).wait_send()

    def own_at(buf, i):
        return buf.at[NC + i // 2, pl.ds((i % 2) * RC, RC)]

    def own_copy(buf, i, send, rs, to_y, to_zh):
        return rcopy(own_at(buf, i), own_at(buf, i), send, rs.at[i], dev(s_id, to_y * 2 + to_zh))

    def own_y(buf, ss, rs):
        return own_copy(buf, c, ss.at[0], rs, (y + 1) % Y, zh)

    def own_wrap(buf, ss, rs):
        return own_copy(buf, c, ss.at[1], rs, Y - 1, zh)

    def own_forward(buf, ss, rs):
        return own_copy(buf, c - 2, ss.at[2], rs, (y + 1) % Y, zh)

    def own_z(buf, zs, rs, yy):
        return own_copy(buf, yy * 2 + zh, zs.at[yy], rs, y, 1 - zh)

    def own_got(buf, rs, i):
        return rcopy(own_at(buf, i), own_at(buf, i), rs.at[i], rs.at[i], sibling)

    def own_start(buf, ss, zs, rs):
        @pl.when(y < Y - 1)
        def _():
            own_y(buf, ss, rs).start()

        if Y > 2:
            @pl.when(y == 0)
            def _():
                own_wrap(buf, ss, rs).start()

        @pl.when(zh == 0)
        def _():
            own_z(buf, zs, rs, y).start()

    def own_next(buf, ss, zs, rs):
        @pl.when(y >= 1)
        def _():
            own_got(buf, rs, c - 2).wait_recv()

            @pl.when(y < Y - 1)
            def _():
                own_forward(buf, ss, rs).start()

            own_z(buf, zs, rs, y - 1).start()

    def own_rest(buf, zs, rs):
        @pl.loop(0, jnp.maximum(y - 1, 0))
        def _(yy):
            own_got(buf, rs, yy * 2 + zh).wait_recv()
            own_z(buf, zs, rs, yy).start()

    def own_end(buf, ss, zs, rs):
        @pl.when(y < Y - 1)
        def _():
            own_y(buf, ss, rs).wait_send()

        if Y > 2:
            @pl.when(y == 0)
            def _():
                own_wrap(buf, ss, rs).wait_send()

        @pl.when((y >= 1) & (y < Y - 1))
        def _():
            own_forward(buf, ss, rs).wait_send()

        @pl.loop(0, y + 1 - zh)
        def _(yy):
            own_z(buf, zs, rs, yy).wait_send()

    barrier = pltpu.get_barrier_semaphore()

    def greet(device):
        pl.semaphore_signal(
            barrier, inc=1, device_id=device, device_id_type=pl.DeviceIdType.MESH
        )

    greet(sibling)
    for t in range(1, NC):
        greet(dev(s_id, (c + t) % NC))
    for p in range(1, NC):
        if places[p][1]:
            greet(g_dev(p))
    for t in range(1, NP):
        greet(dev(((pair + t) % NP) * 2 + core, c))

    kall[0] = pk_ref[...]
    vall[0] = pv_ref[...]
    kall[NC + c // 2, pl.ds((c % 2) * RC, RC)] = rk_ref[0]
    vall[NC + c // 2, pl.ds((c % 2) * RC, RC)] = rv_ref[0]

    @pl.when(c % 2 == 0)
    def _():
        kall[NC + c // 2, RC:] = jnp.zeros((RC, DH), bf16)
        vall[NC + c // 2, RC:] = jnp.zeros((RC, DH), bf16)

    pl.semaphore_wait(barrier, 1 + (NC - 1) + NC // 2 + (NP - 1))

    own_start(kall, ok_s, oz_s, ok_r)
    for p in range(1, NC):
        k_send(p).start()

    ones = jnp.ones((8, DH), bf16)

    def delta(gr, o):
        prod = gr.astype(f32) * o.astype(f32)
        hi = prod.astype(bf16)
        lo = (prod - hi.astype(f32)).astype(bf16)
        return dot(ones, hi, NT) + dot(ones, lo, NT)

    for h in range(H):
        cols = slice(h * DH, (h + 1) * DH)
        rows = slice(h * RC, (h + 1) * RC)
        q[rows] = rq_ref[0, :, cols]
        g[rows] = rg_ref[0, :, cols]
        qp[h * PR : (h + 1) * PR] = pq_ref[:, cols]
        gp[h * PR : (h + 1) * PR] = pg_ref[:, cols]
        D[:, rows] = delta(rg_ref[0, :, cols], ro_ref[0, :, cols])
    prod_o = jnp.concatenate([po_ref[:, h * DH : (h + 1) * DH] for h in range(H)], axis=0)
    Dp[...] = delta(gp[...], prod_o)
    M2[...] = jnp.full_like(M2, MASKED)
    S[...] = jnp.zeros_like(S)
    M2p[...] = jnp.full_like(M2p, MASKED)
    Sp[...] = jnp.zeros_like(Sp)
    dqt[...] = jnp.zeros_like(dqt)
    dqtp[...] = jnp.zeros_like(dqtp)

    def first(i_id, buf, h):
        cols = slice(h * RC, (h + 1) * RC)
        s = dot(kall[i_id], q[cols], NT)
        buf[:, cols] = s
        M2[0, :, cols] = jnp.maximum(
            M2[0, :, cols], jnp.max(s.reshape(KC // 8, 8, RC), axis=0)
        )

    def second(i_id, buf, h):
        cols = slice(h * RC, (h + 1) * RC)
        s = buf[:, cols].reshape(KC // 8, 8, RC)
        new, old = M2[1, :, cols], M2[2, :, cols]
        e = jnp.exp2((s - new) * C)
        S[:, cols] = S[:, cols] * jnp.exp2((old - new) * C) + jnp.sum(e, axis=0)
        E[pl.ds(pl.multiple_of(i_id * KC, KC), KC), cols] = e.reshape(KC, RC).astype(bf16)

    def rotate(i_id):
        M2[2] = M2[1]
        M2[1] = M2[0]
        Mj[i_id] = M2[0]

    values_e = (vall, 1, vs_s, vs_r, vx_s, vx_r, vf_s, vf_r)

    def hand(p):
        mine_ = kall.at[p, half]
        rcopy(mine_, mine_, ks_s.at[p], ks_r.at[p], sibling).wait_recv()
        k_hand(p).start()

    def handed(p):
        part = kall.at[p, other]
        rcopy(part, part, kf_s.at[p], kf_r.at[p], sibling).wait_recv()

    def step(a, b, bufa, bufb):
        for h in range(H):
            first(b, bufb, h)
            second(a, bufa, h)
        rotate(b)

    def own_weights(i_id, mask):
        for h in range(H):
            cols = slice(h * RC, (h + 1) * RC)
            s = dot(kall[i_id], q[cols], NT)
            if mask is not None:
                s = jnp.where(mask, s, MASKED)
            s = s.reshape(KC // 8, 8, RC)
            old = M2[0, :, cols]
            new = jnp.maximum(old, jnp.max(s, axis=0))
            e = jnp.exp2((s - new) * C)
            if mask is not None:
                e = jnp.where(mask.reshape(KC // 8, 8, RC), e, 0.0)
            S[:, cols] = S[:, cols] * jnp.exp2((old - new) * C) + jnp.sum(e, axis=0)
            E[pl.ds(pl.multiple_of(i_id * KC, KC), KC), cols] = e.reshape(KC, RC).astype(bf16)
            Mj[i_id, :, cols] = new
            M2[0, :, cols] = new

    @pl.when(c % 2 == 1)
    def _():
        own_got(kall, ok_r, c - 1).wait_recv()

    dg = NC + y
    key_at = lax.broadcasted_iota(jnp.int32, (KC, RC), 0)
    row_at = lax.broadcasted_iota(jnp.int32, (KC, RC), 1) + zh * RC
    own_weights(dg, key_at <= row_at)
    M2[1] = M2[0]
    for h in range(H):
        first(0, SA, h)
    rotate(0)
    hand(1)

    @pl.loop(0, NC // 2 - 1)
    def _(t):
        p = 2 * t

        @pl.when(t == NC // 2 - 2)
        def _():
            own_next(kall, ok_s, oz_s, ok_r)
            for r in range(1, NC):
                e_send(vall, vs_s, vs_r, r).start()

        hand(p + 2)
        handed(p + 1)
        step(p, p + 1, SA, SB)
        hand(p + 3)
        handed(p + 2)
        step(p + 1, p + 2, SB, SA)

    own_rest(kall, oz_s, ok_r)
    handed(NC - 1)
    step(NC - 2, NC - 1, SA, SB)
    for h in range(H):
        second(NC - 1, SB, h)

    e_share(*values_e)
    own_start(vall, ov_s, ow_s, ov_r)

    @pl.loop(0, jd + 1)
    def _(j):
        s = dot(kall[r_of(j)], qp[...], NT)
        keys = j * KC + lax.broadcasted_iota(jnp.int32, (KC, NPC), 0)
        rows = row0 + lax.broadcasted_iota(jnp.int32, (KC, NPC), 1) % PR
        ok = (keys <= rows).reshape(KC // 8, 8, NPC)
        s = jnp.where(ok, s.reshape(KC // 8, 8, NPC), MASKED)
        old = M2p[...]
        new = jnp.maximum(old, jnp.max(s, axis=0))
        e = jnp.where(ok, jnp.exp2((s - new) * C), 0.0)
        Sp[...] = Sp[...] * jnp.exp2((old - new) * C) + jnp.sum(e, axis=0)
        Ep[pl.ds(pl.multiple_of(j * KC, KC), KC)] = e.reshape(KC, NPC).astype(bf16)
        Mjp[j] = new
        M2p[...] = new

    @pl.loop(0, y)
    def _(jo):
        own_got(kall, ok_r, 2 * jo + 1 - zh).wait_recv()
        own_weights(NC + jo, None)

    e_pass_on(vall, 1, vx_s, vx_r, vf_s, vf_r)
    own_next(vall, ov_s, ow_s, ov_r)

    length = len_ref[0]
    live = (c * RC + lax.broadcasted_iota(jnp.int32, (1, NR), 1) % RC) < length
    m = M2[0]
    mt = jnp.max(m, axis=0, keepdims=True)
    st = jnp.sum(S[...] * jnp.exp2((m - mt) * C), axis=0, keepdims=True)
    Mt[...] = mt
    Inv[...] = jnp.where(live, 1.0 / st, 0.0)
    mp = M2p[...]
    mpt = jnp.max(mp, axis=0, keepdims=True)
    invp = 1.0 / jnp.sum(Sp[...] * jnp.exp2((mp - mpt) * C), axis=0, keepdims=True)

    def grads(i_id, between=None):
        base = pl.ds(pl.multiple_of(i_id * KC, KC), KC)
        for h in range(H):
            cols = slice(h * RC, (h + 1) * RC)
            dp = dot(vall[i_id], g[cols], NT)
            w = jnp.exp2((Mj[i_id, :, cols] - Mt[:, cols]) * C) * Inv[:, cols]
            p = (E[base, cols].astype(f32).reshape(KC // 8, 8, RC) * w).astype(bf16)
            p = p.reshape(KC, RC)
            PB[:, cols] = p
            GB[:, cols] = (dp - D[0:1, cols]).astype(bf16) * p
        if between is not None:
            between()
        DKV[1] = dot(PB[...], g[...], NN)
        DKV[0] = dot(GB[...], q[...], NN)
        for h in range(H):
            cols = slice(h * RC, (h + 1) * RC)
            dqt[h] += dot(kall[i_id], GB[:, cols], TN)

    def grads_prompt(j):
        base = pl.ds(pl.multiple_of(j * KC, KC), KC)
        r = r_of(j)
        dp = dot(vall[r], gp[...], NT)
        w = jnp.exp2((Mjp[j] - mpt) * C) * invp
        p = (Ep[base].astype(f32).reshape(KC // 8, 8, NPC) * w).astype(bf16).reshape(KC, NPC)
        ds = (dp - Dp[0:1]).astype(bf16) * p
        DKV[1] += dot(p, gp[...], NN)
        DKV[0] += dot(ds, qp[...], NN)
        dqtp[...] += dot(kall[r], ds, TN)

    e_arrive(vall, 1, vf_s, vf_r)

    def sib_copy(i):
        return rcopy(sibs.at[i], sibr.at[i], sib_s.at[i], sib_r.at[i], sibling)

    def x_send(i):
        to = ((pair + 1 + i) % NP) * 2 + core
        return rcopy(xs.at[i], xr.at[pair], x_s.at[i], x_r.at[pair], dev(to, c))

    mine = pl.ds(zh * RC, RC)
    theirs = pl.ds((1 - zh) * RC, RC)

    def oy_send(jo):
        return rcopy(oy.at[jo], oyr.at[y], oy_s.at[jo], oy_r.at[y], dev(s_id, jo * 2 + zh))

    def oz_send():
        return rcopy(
            os_.at[0], os_.at[1], o_s.at[0], o_r.at[0], dev(s_id, y * 2 + 1 - zh)
        )

    @pl.loop(0, NP)
    def _(i):
        j = (pair + 1 + i) % NP
        grads(r_of(j))

        @pl.when(j <= jd)
        def _():
            grads_prompt(j)

        @pl.when(i == 0)
        def _():
            own_rest(vall, ow_s, ov_r)

        keep[i, 0] = DKV[0, half] * scaling
        keep[i, 1] = DKV[1, half]
        sibs[i, 0] = (DKV[0, other] * scaling).astype(bf16)
        sibs[i, 1] = DKV[1, other].astype(bf16)
        sib_copy(i).start()

        @pl.when(i >= 1)
        def _():
            sib_copy(i - 1).wait_recv()
            xs[i - 1] = (keep[i - 1] + sibr[i - 1].astype(f32)).astype(bf16)
            x_send(i - 1).start()

        @pl.when((i >= 2) & (i < y + 2))
        def _():
            jo = i - 2
            own_got(vall, ov_r, 2 * jo + 1 - zh).wait_recv()
            grads(NC + jo)
            oy[jo, 0] = (DKV[0] * scaling).astype(bf16)
            oy[jo, 1] = DKV[1].astype(bf16)
            oy_send(jo).start()

    def c_send(t):
        to = (c + t) % NC
        return rcopy(cs.at[t], cr.at[c], c_s.at[t], c_r.at[c], dev(s_id, to))

    def sum_prompt():
        sib_copy(NP - 1).wait_recv()
        total = keep[NP - 1] + sibr[NP - 1].astype(f32)
        for t in range(1, NP):
            k = (pair + t) % NP
            rcopy(xr.at[k], xr.at[k], x_s.at[t - 1], x_r.at[k], sibling).wait_recv()
            total = total + xr[k].astype(f32)
        keep[NP - 1] = total

        for t in range(1, NC):
            to = (c + t) % NC
            cs[t] = keep[NP - 1, :, pl.ds(to * PR, PR)].astype(bf16)
            c_send(t).start()

    @pl.when(zh == 1)
    def _():
        own_got(vall, ov_r, c - 1).wait_recv()

    grads(dg, sum_prompt)
    own_keep[0] = DKV[0] * scaling
    own_keep[1] = DKV[1]

    @pl.loop(y + 1, Y)
    def _(yy):
        rcopy(oyr.at[yy], oyr.at[yy], oy_s.at[yy], oy_r.at[yy], sibling).wait_recv()
        own_keep[...] += oyr[yy].astype(f32)

    os_[0] = own_keep[:, theirs].astype(bf16)
    oz_send().start()

    for h in range(H):
        cols = slice(h * DH, (h + 1) * DH)
        drq_ref[0, :, cols] = (dqt[h].T * scaling).astype(bf16)
    dqp = (dqtp[...].T * scaling).astype(bf16)
    for h in range(H):
        dpq_ref[:, h * DH : (h + 1) * DH] = dqp[h * PR : (h + 1) * PR]

    oz_send().wait_recv()
    total = own_keep[:, mine] + os_[1].astype(f32)
    drk_ref[0] = total[0].astype(bf16)
    drv_ref[0] = total[1].astype(bf16)

    total = keep[NP - 1, :, pl.ds(c * PR, PR)]
    for t in range(1, NC):
        k = (c + t) % NC
        rcopy(cr.at[k], cr.at[k], c_s.at[t], c_r.at[k], sibling).wait_recv()
        total = total + cr[k].astype(f32)
    dpk_ref[...] = total[0].astype(bf16)
    dpv_ref[...] = total[1].astype(bf16)

    for r in range(1, NC):
        c_send(r).wait_send()
    for p in range(1, NC):
        k_send(p).wait_send()
        k_hand(p).wait_send()
    e_end(*values_e)
    own_end(kall, ok_s, oz_s, ok_r)
    own_end(vall, ov_s, ow_s, ov_r)
    oz_send().wait_send()

    @pl.loop(0, y)
    def _(jo):
        oy_send(jo).wait_send()

    for i in range(NP):
        sib_copy(i).wait_send()
    for i in range(NP - 1):
        x_send(i).wait_send()


def copy_kernel(*refs):
    for i in range(6):
        refs[6 + i][...] = refs[i][...]


def on_device(NS, NC, *args):
    pq, pk = args[0], args[1]
    rq = args[5]
    DH = pk.shape[1]
    H = pq.shape[1] // DH
    KC, PR, RC = pk.shape[0], pq.shape[0], rq.shape[1]
    NR, NPC, NP, NK = RC * H, PR * H, NS // 2, NC + NC // 2
    vm = pltpu.VMEM
    dma = pltpu.SemaphoreType.DMA
    sds = jax.ShapeDtypeStruct
    scratch = [
        vm((NR, DH), bf16), vm((NR, DH), bf16), vm((NPC, DH), bf16), vm((NPC, DH), bf16),
        vm((NK, KC, DH), bf16), vm((NK, KC, DH), bf16),
        vm((NK * KC, NR), bf16), vm((NC * KC, NPC), bf16),
        vm((KC, NR), f32), vm((KC, NR), f32), vm((KC, NR), bf16), vm((KC, NR), bf16),
        vm((8, 128), bf16), vm((8, 128), bf16),
        vm((3, 8, NR), f32), vm((8, NR), f32), vm((NK, 8, NR), f32), vm((1, NR), f32),
        vm((1, NR), f32), vm((8, NR), f32),
        vm((8, NPC), f32), vm((8, NPC), f32), vm((NC, 8, NPC), f32), vm((8, NPC), f32),
        vm((H, DH, RC), f32), vm((DH, NPC), f32), vm((2, KC, DH), f32),
        vm((NP, 2, RC, DH), f32), vm((NP, 2, RC, DH), bf16), vm((NP, 2, RC, DH), bf16),
        vm((NP, 2, RC, DH), bf16), vm((NP, 2, RC, DH), bf16),
        vm((NC, 2, PR, DH), bf16), vm((NC, 2, PR, DH), bf16),
        vm((2, KC, DH), f32), vm((2, 2, RC, DH), bf16),
        vm((NC // 2, 2, KC, DH), bf16), vm((NC // 2, 2, KC, DH), bf16),
    ]
    scratch += [dma((NC,))] * 16 + [dma((NP,))] * 4 + [dma((NC,))] * 6
    vspec = pl.BlockSpec(memory_space=pltpu.VMEM)
    outs = pl.pallas_call(
        functools.partial(kernel, NS, NC, H, KC, PR),
        out_shape=(
            sds((PR, H * DH), bf16), sds((PR, DH), bf16), sds((PR, DH), bf16),
            sds((1, RC, H * DH), bf16), sds((1, RC, DH), bf16), sds((1, RC, DH), bf16),
        ),
        in_specs=[vspec] * 10 + [pl.BlockSpec(memory_space=pltpu.SMEM)],
        out_specs=[vspec] * 6,
        scratch_shapes=scratch,
        compiler_params=pltpu.CompilerParams(
            collective_id=0, has_side_effects=True, vmem_limit_bytes=62 * 2**20
        ),
    )(*args)
    return pl.pallas_call(
        copy_kernel,
        out_shape=tuple(sds(o.shape, o.dtype) for o in outs),
        in_specs=[vspec] * 6,
        out_specs=[vspec] * 6,
    )(*outs)


def solution(mesh):
    placed = (
        P(("sample", "ctx"), None),
        P("ctx", None),
        P("ctx", None),
        P(("sample", "ctx"), None),
        P(("sample", "ctx"), None),
        P("sample", "ctx", None),
        P("sample", "ctx", None),
        P("sample", "ctx", None),
        P("sample", "ctx", None),
        P("sample", "ctx", None),
        P("sample"),
    )
    return jax.shard_map(
        functools.partial(on_device, mesh.shape["sample"], mesh.shape["ctx"]),
        mesh=mesh,
        in_specs=placed,
        out_specs=(
            P(("sample", "ctx"), None),
            P(("sample", "ctx"), None),
            P(("sample", "ctx"), None),
            P("sample", "ctx", None),
            P("sample", "ctx", None),
            P("sample", "ctx", None),
        ),
        check_vma=False,
    )
```
